512 devices in a mesh: blk: 256 (over y, x_lo, z, core), dp: 2 (over x_hi).
Axes of the slice: x: 4 (x_hi: 2, x_lo: 2; x = x_hi * 2 + x_lo), y: 8, z: 8, core: 2. Of those that a mesh axis runs over, the one named last changes fastest.
Arguments:
- teacher_rows: bfloat16 [8192, 256], P('blk', 'dp'), may hold values from -6 to 6
- teacher_gate: bfloat16 [26624, 8192], P('blk', 'dp'), may hold values from -0.0625 to 0.0625
- teacher_up: bfloat16 [26624, 8192], P('blk', 'dp'), may hold values from -0.0625 to 0.0625
- teacher_down: bfloat16 [26624, 8192], P('blk', 'dp'), may hold values from -0.15625 to 0.15625
- student_rows: bfloat16 [8192, 256], P('blk', 'dp'), may hold values from -6 to 6
- projector: bfloat16 [8192, 8192], P('blk'), may hold values from -0.0625 to 0.0625
Outputs:
- teacher_hidden: bfloat16 [26624, 256], P('blk', 'dp')
- residual_error: bfloat16 [8192, 256], P('blk', 'dp')
- grad_projector: bfloat16 [8192, 8192], P('blk')
The draws below stay inside these ranges and needn't reach their ends.
All inputs are finite; a program needn't handle non-finite values.
Results may differ from the reference program's by a relative error of at most 0.012.
Values may be sent and summed in bfloat16 or wider, within the bound.
No kernel may reach another device: no remote copies, remote signals or barrier semaphores. Data moves between devices by JAX's collectives and lax.ppermute only.
A program may use at most 64 MiB of HBM per device.

```python
import jax
import jax.numpy as jnp

DT = 8192
HID = 26624
DS = 8192
TOKALL = 256


def strengthened(entries, rng, source, target, parts, factor):
    owner, partner = [(jnp.arange(entries.shape[dim]) // (entries.shape[dim] // parts)).reshape([-1 if axis == dim else 1 for axis in range(entries.ndim)]) for dim in (source, target)]
    chosen = jax.random.permutation(rng, parts)[partner]
    strong = (owner == chosen) | (owner == (partner + parts // 2) % parts)
    return jnp.where(strong, factor * entries, entries)


def levels(stream_key, shape, shards, low, largest):
    def one(position, parts):
        steps = jax.random.uniform(jax.random.fold_in(jax.random.fold_in(stream_key, 6), position), (parts,), jnp.float32, low / len(shards), largest / len(shards))
        return jnp.repeat(jnp.exp(steps), shape[position] // parts).reshape((-1,) + (1,) * (len(shape) - position - 1))

    level = one(*shards[0])
    for cut in shards[1:]:
        level = level * one(*cut)
    return level


def noise(rng, dims, spread, bound, split=(), held_as=jnp.bfloat16):
    array = jax.random.normal(rng, dims, jnp.float32) * spread
    if len(split) > 0:
        array = levels(rng, dims, split, -0.22, 0.18) * array
    return jnp.clip(array, min=-bound, max=bound).astype(held_as)


def gaussian_with(key, dims, deviation, reach, shards, heavy, kind=jnp.bfloat16):
    values = deviation * jax.random.normal(key, dims, jnp.float32)
    if shards:
        values = values * levels(key, dims, shards, -0.22, 0.18)
    return jnp.clip(strengthened(values, jax.random.fold_in(key, 3), *heavy), -reach, reach).astype(kind)


def setup_inputs(seed: int = 0) -> dict:
    arg_keys = jax.random.split(jax.random.key(seed), 7)
    teacher_rows = noise(arg_keys[0], (DT, TOKALL), 1.0, 6.0, ((0, 256), (1, 2)))
    teacher_gate = noise(arg_keys[1], (HID, DT), DT ** -0.5, 0.0625, ((0, 256), (1, 2)))
    teacher_up = noise(arg_keys[2], (HID, DT), DT ** -0.5, 0.0625, ((0, 256), (1, 2)))
    teacher_down = gaussian_with(arg_keys[3], (HID, DT), HID ** -0.5, 0.15625, ((0, 256), (1, 2)), (0, 1, 256, 6.0))
    student_rows = noise(arg_keys[4], (DS, TOKALL), 1.0, 6.0, ((0, 256), (1, 2)))
    projector = noise(arg_keys[5], (DT, DS), DS ** -0.5, 0.0625, ((0, 256),))
    return {"teacher_rows": teacher_rows, "teacher_gate": teacher_gate, "teacher_up": teacher_up, "teacher_down": teacher_down, "student_rows": student_rows, "projector": projector}


def reference(teacher_rows, teacher_gate, teacher_up, teacher_down, student_rows, projector):
    preact = jnp.dot(teacher_gate, teacher_rows, preferred_element_type=jnp.float32)
    uppre = jnp.dot(teacher_up, teacher_rows, preferred_element_type=jnp.float32)
    teacher_hidden = (jax.nn.silu(preact) * uppre).astype(jnp.bfloat16)
    teacher_out = jnp.dot(teacher_down.T, teacher_hidden, preferred_element_type=jnp.float32)
    student_out = jnp.dot(projector, student_rows, preferred_element_type=jnp.float32)
    residual_error = (student_out - teacher_out).astype(jnp.bfloat16)
    grad_projector = jnp.dot(residual_error, student_rows.T, preferred_element_type=jnp.float32).astype(jnp.bfloat16)
    return teacher_hidden, residual_error, grad_projector
```

```python
import functools

import jax
import jax.numpy as jnp
from jax import lax
from jax.experimental import pallas as pl
from jax.experimental.pallas import tpu as pltpu
from jax.sharding import Mesh, PartitionSpec as P

CHIPS = ("y", "x", "z")
SWAP = [(0, 1), (1, 0)]
F32, BF16 = jnp.float32, jnp.bfloat16
PARAMS = pltpu.CompilerParams(vmem_limit_bytes=24 << 20)


def cost(flops, size):
    return pl.CostEstimate(flops=flops, bytes_accessed=size, transcendentals=0)


def zip_cores(core, own, other):
    count, rows, tokens = own.shape
    even = jnp.where(core == 0, own, other)
    odd = jnp.where(core == 0, other, own)
    return jnp.stack([even, odd], axis=1).reshape(count * 2 * rows, tokens)


def copies_kernel(rows_ref, _, out_ref):
    out_ref[...] = jnp.broadcast_to(rows_ref[...][None], out_ref.shape)


def copies(rows, after, count):
    return pl.pallas_call(
        copies_kernel,
        in_specs=[pl.BlockSpec(memory_space=pltpu.VMEM), pl.BlockSpec(memory_space=pl.ANY)],
        out_shape=jax.ShapeDtypeStruct((count, *rows.shape), rows.dtype),
        compiler_params=PARAMS,
        cost_estimate=cost(0, count * rows.size * 2),
        name="copies",
    )(rows, after)


def up_kernel(place_ref, own_ref, other_ref, gate_ref, up_ref, keep_ref, send_ref, acc_ref):
    step, last = pl.program_id(0), pl.num_programs(0) - 1
    core, half = place_ref[0], place_ref[1]

    @pl.when(step == 0)
    def _():
        acc_ref[...] = jnp.zeros_like(acc_ref)

    tokens = own_ref.shape[-1]
    rows = jnp.concatenate(
        [zip_cores(core, own_ref[t], other_ref[t]) for t in range(2)], axis=1
    )
    for i, ref in enumerate((gate_ref, up_ref)):
        acc_ref[i] += jnp.dot(ref[...], rows, preferred_element_type=F32)

    @pl.when(step == last)
    def _():
        for i in range(2):
            low, high = acc_ref[i, :, :tokens], acc_ref[i, :, tokens:]
            keep_ref[i] = jnp.where(half == 0, low, high)
            send_ref[i] = jnp.where(half == 0, high, low).astype(BF16)


def up_part(place, own, other, gate, up, steps=4):
    hidden, width = gate.shape
    rows, tokens = own.shape[-2:]
    per = width // (2 * rows * steps)
    own, other = (a.reshape(2, -1, rows, tokens) for a in (own, other))
    block = pl.BlockSpec((2, per, rows, tokens), lambda k, _: (0, k, 0, 0))
    weight = pl.BlockSpec((hidden, width // steps), lambda k, _: (0, k))
    whole = pl.BlockSpec((2, hidden, tokens), lambda k, _: (0, 0, 0))
    return pl.pallas_call(
        up_kernel,
        grid_spec=pltpu.PrefetchScalarGridSpec(
            num_scalar_prefetch=1,
            grid=(steps,),
            in_specs=[block, block, weight, weight],
            out_specs=[whole, whole],
            scratch_shapes=[pltpu.VMEM((2, hidden, 2 * tokens), F32)],
        ),
        out_shape=[
            jax.ShapeDtypeStruct((2, hidden, tokens), F32),
            jax.ShapeDtypeStruct((2, hidden, tokens), BF16),
        ],
        compiler_params=PARAMS,
        cost_estimate=cost(8 * hidden * width * tokens, 4 * hidden * width + 4 * own.size),
        name="gate_up",
    )(place, own, other, gate, up)


def down_kernel(place_ref, keep_ref, got_ref, near_ref, far_ref, hidden_ref, mine_ref, theirs_ref):
    side, step = pl.program_id(0), pl.program_id(1)
    core = place_ref[0]

    @pl.when((side == 0) & (step == 0))
    def _():
        preact, uppre = (keep_ref[i] + got_ref[i].astype(F32) for i in range(2))
        hidden_ref[...] = (preact / (1 + jnp.exp(-preact)) * uppre).astype(BF16)

    def part(ref):
        out = lax.dot_general(
            ref[...], hidden_ref[...], (((0,), (0,)), ((), ())), preferred_element_type=F32
        ).astype(BF16)
        count, rows, tokens = mine_ref.shape[1:]
        out = out.reshape(count, 2, rows, tokens)
        even, odd = out[:, 0], out[:, 1]
        mine_ref[0] = jnp.where(core == 0, even, odd)
        theirs_ref[0] = jnp.where(core == 0, odd, even)

    pl.when(side == 0)(lambda: part(near_ref))
    pl.when(side == 1)(lambda: part(far_ref))


def down_part(place, keep, got, near, far, rows, steps=4):
    hidden, width = near.shape
    tokens = keep.shape[-1]
    count = width // (2 * rows)
    whole = pl.BlockSpec((2, hidden, tokens), lambda s, k, _: (0, 0, 0))
    block = pl.BlockSpec(
        (1, count // steps, rows, tokens), lambda s, k, p: ((s + p[1]) % 2, k, 0, 0)
    )
    out = jax.ShapeDtypeStruct((2, count, rows, tokens), BF16)
    hidden_units, mine, theirs = pl.pallas_call(
        down_kernel,
        grid_spec=pltpu.PrefetchScalarGridSpec(
            num_scalar_prefetch=1,
            grid=(2, steps),
            in_specs=[
                whole,
                whole,
                pl.BlockSpec((hidden, width // steps), lambda s, k, _: (0, jnp.where(s == 0, k, steps - 1))),
                pl.BlockSpec((hidden, width // steps), lambda s, k, _: (0, jnp.where(s == 1, k, 0))),
            ],
            out_specs=[pl.BlockSpec((hidden, tokens), lambda s, k, _: (0, 0)), block, block],
        ),
        out_shape=[jax.ShapeDtypeStruct((hidden, tokens), BF16), out, out],
        compiler_params=PARAMS,
        cost_estimate=cost(4 * hidden * width * tokens, 4 * hidden * width + 8 * width * tokens),
        name="down",
    )(place, keep, got, near, far)
    return hidden_units, *(a.reshape(2 * count, rows, tokens) for a in (mine, theirs))


def student_kernel(place_ref, own_ref, other_ref, projector_ref, all_ref, out_ref):
    rows = zip_cores(place_ref[0], own_ref[...], other_ref[...])
    all_ref[...] = rows
    part = jnp.dot(projector_ref[...], rows, preferred_element_type=F32)

    @pl.when(pl.program_id(0) == 0)
    def _():
        out_ref[...] = part

    @pl.when(pl.program_id(0) != 0)
    def _():
        out_ref[...] += part


def student_part(place, own, other, projector, steps=8):
    count, rows, tokens = own.shape
    mine, width = projector.shape
    block = pl.BlockSpec((count // steps, rows, tokens), lambda k, _: (k, 0, 0))
    return pl.pallas_call(
        student_kernel,
        grid_spec=pltpu.PrefetchScalarGridSpec(
            num_scalar_prefetch=1,
            grid=(steps,),
            in_specs=[block, block, pl.BlockSpec((mine, width // steps), lambda k, _: (0, k))],
            out_specs=[
                pl.BlockSpec((width // steps, tokens), lambda k, _: (k, 0)),
                pl.BlockSpec((mine, tokens), lambda k, _: (0, 0)),
            ],
        ),
        out_shape=[
            jax.ShapeDtypeStruct((width, tokens), BF16),
            jax.ShapeDtypeStruct((mine, tokens), F32),
        ],
        compiler_params=PARAMS,
        cost_estimate=cost(2 * mine * width * tokens, 4 * width * tokens + 2 * mine * width),
        name="student",
    )(place, own, other, projector)


def grad_kernel(terms_ref, student_out_ref, student_ref, residual_ref, grad_ref):
    @pl.when(pl.program_id(0) == 0)
    def _():
        teacher_out = jnp.sum(terms_ref[...].astype(F32), axis=0)
        residual_ref[...] = (student_out_ref[...] - teacher_out).astype(BF16)

    grad_ref[...] = lax.dot_general(
        residual_ref[...], student_ref[...], (((1,), (1,)), ((), ())), preferred_element_type=F32
    ).astype(BF16)


def grad_part(terms, student_out, student_all, steps=4):
    rows, tokens = student_out.shape
    width = student_all.shape[0]
    small = pl.BlockSpec((rows, tokens), lambda k: (0, 0))
    return pl.pallas_call(
        grad_kernel,
        grid=(steps,),
        in_specs=[
            pl.BlockSpec(terms.shape, lambda k: (0, 0, 0)),
            small,
            pl.BlockSpec((width // steps, tokens), lambda k: (k, 0)),
        ],
        out_specs=[small, pl.BlockSpec((rows, width // steps), lambda k: (0, k))],
        out_shape=[
            jax.ShapeDtypeStruct((rows, tokens), BF16),
            jax.ShapeDtypeStruct((rows, width), BF16),
        ],
        compiler_params=PARAMS,
        cost_estimate=cost(2 * rows * width * tokens, 2 * (terms.size + width * tokens + rows * width)),
        name="gradient",
    )(terms, student_out, student_all)


def shards(teacher_rows, teacher_gate, teacher_up, teacher_down, student_rows, projector):
    place = jnp.stack([lax.axis_index("core"), lax.axis_index("dp")]).astype(jnp.int32)
    rows = teacher_rows.shape[0]
    chips = lax.axis_size(CHIPS)
    across = lax.axis_size("y") // 2
    spread = functools.partial(
        lax.all_to_all, axis_name=CHIPS, split_axis=0, concat_axis=0, tiled=True
    )

    trade = []
    for y in range(across):
        low, high = 2 * y, 2 * (y + across)
        trade += [(low, low), (low + 1, high), (high, low + 1), (high + 1, high + 1)]
    held = lax.ppermute(teacher_rows, ("y", "dp"), trade)
    teacher_own = spread(copies(held, held, chips))
    teacher_other = lax.ppermute(teacher_own, "core", SWAP)
    down_far = lax.ppermute(teacher_down, "dp", SWAP)

    student_own = spread(copies(student_rows, teacher_own, chips))

    keep, send = up_part(place, teacher_own, teacher_other, teacher_gate, teacher_up)
    got = lax.ppermute(send, "dp", SWAP)
    teacher_hidden, mine, theirs = down_part(place, keep, got, teacher_down, down_far, rows)
    chip_sum = (
        mine.astype(F32) + lax.ppermute(theirs, "core", SWAP).astype(F32)
    ).astype(BF16)
    terms = spread(chip_sum)

    student_other = lax.ppermute(student_own, "core", SWAP)
    student_all, student_out = student_part(place, student_own, student_other, projector)
    residual_error, grad_local = grad_part(terms, student_out, student_all)
    grad_projector = grad_local + lax.ppermute(grad_local, "dp", SWAP)
    return (teacher_hidden, residual_error, grad_projector)


def solution(mesh):
    fine = Mesh(mesh.devices.reshape(8, 2, 8, 2, 2), (*CHIPS, "core", "dp"))
    blk = (*CHIPS, "core")
    return jax.shard_map(
        shards,
        mesh=fine,
        in_specs=(P(blk, "dp"),) * 5 + (P(blk, None),),
        out_specs=(P(blk, "dp"), P(blk, "dp"), P(blk, None)),
        check_vma=False,
    )
```

```python
import functools

import jax
import jax.numpy as jnp
from jax import lax
from jax.experimental import pallas as pl
from jax.experimental.pallas import tpu as pltpu
from jax.sharding import Mesh, PartitionSpec as P

CHIPS = ("y", "x", "z")
SWAP = [(0, 1), (1, 0)]
F32, BF16 = jnp.float32, jnp.bfloat16
PARAMS = pltpu.CompilerParams(vmem_limit_bytes=24 << 20)


def cost(flops, size):
    return pl.CostEstimate(flops=flops, bytes_accessed=size, transcendentals=0)


def zip_cores(core, own, other):
    count, rows, tokens = own.shape
    even = jnp.where(core == 0, own, other)
    odd = jnp.where(core == 0, other, own)
    return jnp.stack([even, odd], axis=1).reshape(count * 2 * rows, tokens)


def copies_kernel(rows_ref, _, out_ref):
    out_ref[...] = jnp.broadcast_to(rows_ref[...][None], out_ref.shape)


def copies(rows, after, count):
    return pl.pallas_call(
        copies_kernel,
        in_specs=[pl.BlockSpec(memory_space=pltpu.VMEM), pl.BlockSpec(memory_space=pl.ANY)],
        out_shape=jax.ShapeDtypeStruct((count, *rows.shape), rows.dtype),
        compiler_params=PARAMS,
        cost_estimate=cost(0, count * rows.size * 2),
        name="copies",
    )(rows, after)


def up_kernel(place_ref, own_ref, other_ref, gate_ref, up_ref, keep_ref, send_ref, weight_ref, acc_ref, sem_ref):
    core, half = place_ref[0], place_ref[1]
    steps, width = weight_ref.shape[1], weight_ref.shape[3]
    per, tokens = own_ref.shape[1] // steps, own_ref.shape[3]
    arrive = []
    for k in range(steps):
        for i, ref in enumerate((gate_ref, up_ref)):
            arrive.append(
                pltpu.make_async_copy(ref.at[:, pl.ds(k * width, width)], weight_ref.at[i, k], sem_ref.at[i, k])
            )
            arrive[-1].start()
    for k in range(steps):
        part = slice(k * per, (k + 1) * per)
        rows = jnp.concatenate(
            [zip_cores(core, own_ref[t, part], other_ref[t, part]) for t in range(2)], axis=1
        )
        for i in range(2):
            arrive[2 * k + i].wait()
            term = jnp.dot(weight_ref[i, k], rows, preferred_element_type=F32)
            if k == 0:
                acc_ref[i] = term
            else:
                acc_ref[i] += term
    for i in range(2):
        low, high = acc_ref[i, :, :tokens], acc_ref[i, :, tokens:]
        keep_ref[i] = jnp.where(half == 0, low, high)
        send_ref[i] = jnp.where(half == 0, high, low).astype(BF16)


def up_part(place, own, other, gate, up, steps=4):
    hidden, width = gate.shape
    rows, tokens = own.shape[-2:]
    own, other = (a.reshape(2, -1, rows, tokens) for a in (own, other))
    vmem = pl.BlockSpec(memory_space=pltpu.VMEM)
    hbm = pl.BlockSpec(memory_space=pltpu.HBM)
    return pl.pallas_call(
        up_kernel,
        in_specs=[pl.BlockSpec(memory_space=pltpu.SMEM), vmem, vmem, hbm, hbm],
        out_specs=[vmem, vmem],
        out_shape=[
            jax.ShapeDtypeStruct((2, hidden, tokens), F32),
            jax.ShapeDtypeStruct((2, hidden, tokens), BF16),
        ],
        scratch_shapes=[
            pltpu.VMEM((2, steps, hidden, width // steps), BF16),
            pltpu.VMEM((2, hidden, 2 * tokens), F32),
            pltpu.SemaphoreType.DMA((2, steps)),
        ],
        compiler_params=PARAMS,
        cost_estimate=cost(8 * hidden * width * tokens, 4 * hidden * width + 4 * own.size),
        name="gate_up",
    )(place, own, other, gate, up)


def hidden_kernel(keep_ref, got_ref, out_ref):
    preact, uppre = (keep_ref[i] + got_ref[i].astype(F32) for i in range(2))
    out_ref[...] = (preact / (1 + jnp.exp(-preact)) * uppre).astype(BF16)


def hidden_part(keep, got):
    return pl.pallas_call(
        hidden_kernel,
        out_shape=jax.ShapeDtypeStruct(keep.shape[1:], BF16),
        compiler_params=PARAMS,
        cost_estimate=cost(0, 0),
        name="hidden",
    )(keep, got)


def down_kernel(place_ref, hidden_ref, down_ref, mine_ref, theirs_ref):
    core = place_ref[0]
    count, rows, tokens = mine_ref.shape
    out = jnp.dot(down_ref[...], hidden_ref[...], preferred_element_type=F32).astype(BF16)
    out = out.reshape(count, 2, rows, tokens)
    even, odd = out[:, 0], out[:, 1]
    mine_ref[...] = jnp.where(core == 0, even, odd)
    theirs_ref[...] = jnp.where(core == 0, odd, even)


def down_part(place, hidden_units, down, rows, steps=4):
    width, hidden = down.shape
    tokens = hidden_units.shape[-1]
    count = width // (2 * rows)
    block = pl.BlockSpec((count // steps, rows, tokens), lambda k, _: (k, 0, 0))
    out = jax.ShapeDtypeStruct((count, rows, tokens), BF16)
    return pl.pallas_call(
        down_kernel,
        grid_spec=pltpu.PrefetchScalarGridSpec(
            num_scalar_prefetch=1,
            grid=(steps,),
            in_specs=[
                pl.BlockSpec((hidden, tokens), lambda k, _: (0, 0)),
                pl.BlockSpec((width // steps, hidden), lambda k, _: (k, 0)),
            ],
            out_specs=[block, block],
        ),
        out_shape=[out, out],
        compiler_params=PARAMS,
        cost_estimate=cost(0, 0),
        name="down",
    )(place, hidden_units, down)


def student_kernel(place_ref, own_ref, own_core_ref, next_ref, next_core_ref, projector_ref, all_ref, out_ref):
    core, x = place_ref[0], place_ref[2]
    here = zip_cores(core, own_ref[0], own_core_ref[0])
    there = zip_cores(core, next_ref[0], next_core_ref[0])
    rows = jnp.concatenate([jnp.where(x == 0, here, there), jnp.where(x == 0, there, here)])
    all_ref[...] = rows
    part = jnp.dot(projector_ref[...], rows, preferred_element_type=F32)

    @pl.when(pl.program_id(0) == 0)
    def _():
        out_ref[...] = part

    @pl.when(pl.program_id(0) != 0)
    def _():
        out_ref[...] += part


def student_part(place, pieces, projector):
    steps, count, rows, tokens = pieces[0].shape
    mine, width = projector.shape
    block = pl.BlockSpec((1, count, rows, tokens), lambda k, _: (k, 0, 0, 0))
    return pl.pallas_call(
        student_kernel,
        grid_spec=pltpu.PrefetchScalarGridSpec(
            num_scalar_prefetch=1,
            grid=(steps,),
            in_specs=[block] * 4 + [pl.BlockSpec((mine, width // steps), lambda k, _: (0, k))],
            out_specs=[
                pl.BlockSpec((width // steps, tokens), lambda k, _: (k, 0)),
                pl.BlockSpec((mine, tokens), lambda k, _: (0, 0)),
            ],
        ),
        out_shape=[
            jax.ShapeDtypeStruct((width, tokens), BF16),
            jax.ShapeDtypeStruct((mine, tokens), F32),
        ],
        compiler_params=PARAMS,
        cost_estimate=cost(2 * mine * width * tokens, 4 * width * tokens + 2 * mine * width),
        name="student",
    )(place, *pieces, projector)


def grad_kernel(terms_ref, student_out_ref, student_ref, residual_ref, grad_ref, rows_ref, sem_ref):
    steps, width = rows_ref.shape[:2]
    arrive = []
    for k in range(steps):
        arrive.append(
            pltpu.make_async_copy(student_ref.at[pl.ds(k * width, width)], rows_ref.at[k], sem_ref.at[k])
        )
        arrive[-1].start()
    teacher_out = jnp.sum(terms_ref[...].astype(F32), axis=0)
    residual = (student_out_ref[...] - teacher_out).astype(BF16)
    residual_ref[...] = residual
    for k in range(steps):
        arrive[k].wait()
        grad_ref[:, k * width : (k + 1) * width] = lax.dot_general(
            residual, rows_ref[k], (((1,), (1,)), ((), ())), preferred_element_type=F32
        ).astype(BF16)


def grad_part(terms, student_out, student_all, steps=8):
    rows, tokens = student_out.shape
    width = student_all.shape[0]
    vmem = pl.BlockSpec(memory_space=pltpu.VMEM)
    return pl.pallas_call(
        grad_kernel,
        in_specs=[vmem, vmem, pl.BlockSpec(memory_space=pltpu.HBM)],
        out_specs=[vmem, vmem],
        out_shape=[
            jax.ShapeDtypeStruct((rows, tokens), BF16),
            jax.ShapeDtypeStruct((rows, width), BF16),
        ],
        scratch_shapes=[
            pltpu.VMEM((steps, width // steps, tokens), BF16),
            pltpu.SemaphoreType.DMA((steps,)),
        ],
        compiler_params=PARAMS,
        cost_estimate=cost(2 * rows * width * tokens, 2 * (terms.size + width * tokens + rows * width)),
        name="gradient",
    )(terms, student_out, student_all)


def shards(teacher_rows, teacher_gate, teacher_up, teacher_down, student_rows, projector):
    place = jnp.stack([lax.axis_index(name) for name in ("core", "dp", "x")]).astype(jnp.int32)
    rows = teacher_rows.shape[0]
    chips = lax.axis_size(CHIPS)
    across = lax.axis_size("y") // 2
    spread = functools.partial(lax.all_to_all, split_axis=0, concat_axis=0, tiled=True)

    trade = []
    for y in range(across):
        low, high = 2 * y, 2 * (y + across)
        trade += [(low, low), (low + 1, high), (high, low + 1), (high + 1, high + 1)]
    held = lax.ppermute(teacher_rows, ("y", "dp"), trade)
    down_far = lax.ppermute(teacher_down, "dp", SWAP)
    teacher_own = spread(copies(held, held, chips), CHIPS)
    teacher_own, down_far = lax.optimization_barrier((teacher_own, down_far))
    teacher_other = lax.ppermute(teacher_own, "core", SWAP)

    plane = ("y", "z")
    student_own = spread(copies(student_rows, teacher_own, lax.axis_size(plane)), plane)

    keep, send = up_part(place, teacher_own, teacher_other, teacher_gate, teacher_up)
    got = lax.ppermute(send, "dp", SWAP)
    teacher_hidden = hidden_part(keep, got)
    sums = []
    for down in (teacher_down, down_far):
        mine, theirs = down_part(place, teacher_hidden, down.T, rows)
        sums.append((mine.astype(F32) + lax.ppermute(theirs, "core", SWAP).astype(F32)).astype(BF16))
    near, far = sums
    first = place[1] == 0
    chip_sum = jnp.concatenate([jnp.where(first, near, far), jnp.where(first, far, near)])
    terms = spread(chip_sum, CHIPS)

    student_next = lax.ppermute(student_own, "x", SWAP)
    pieces = []
    for piece in (student_own, student_next):
        pieces += [piece, lax.ppermute(piece, "core", SWAP)]
    pieces = [a.reshape(lax.axis_size("y"), -1, *a.shape[1:]) for a in pieces]
    student_all, student_out = student_part(place, pieces, projector)
    residual_error, grad_local = grad_part(terms, student_out, student_all)
    grad_projector = grad_local + lax.ppermute(grad_local, "dp", SWAP)
    return (teacher_hidden, residual_error, grad_projector)


def solution(mesh):
    fine = Mesh(mesh.devices.reshape(8, 2, 8, 2, 2), (*CHIPS, "core", "dp"))
    blk = (*CHIPS, "core")
    return jax.shard_map(
        shards,
        mesh=fine,
        in_specs=(P(blk, "dp"),) * 5 + (P(blk, None),),
        out_specs=(P(blk, "dp"), P(blk, "dp"), P(blk, None)),
        check_vma=False,
    )
```

```python
import functools

import jax
import jax.numpy as jnp
from jax import lax
from jax.experimental import pallas as pl
from jax.experimental.pallas import tpu as pltpu
from jax.sharding import Mesh, PartitionSpec as P

CHIPS = ("y", "x", "z")
SWAP = [(0, 1), (1, 0)]
F32, BF16 = jnp.float32, jnp.bfloat16
PARAMS = pltpu.CompilerParams(vmem_limit_bytes=24 << 20)


def cost(flops, size):
    return pl.CostEstimate(flops=flops, bytes_accessed=size, transcendentals=0)


def zip_cores(core, own, other):
    count, rows, tokens = own.shape
    even = jnp.where(core == 0, own, other)
    odd = jnp.where(core == 0, other, own)
    return jnp.stack([even, odd], axis=1).reshape(count * 2 * rows, tokens)


def copies_kernel(rows_ref, _, out_ref):
    out_ref[...] = jnp.broadcast_to(rows_ref[...][None], out_ref.shape)


def copies(rows, after, count):
    return pl.pallas_call(
        copies_kernel,
        in_specs=[pl.BlockSpec(memory_space=pltpu.VMEM), pl.BlockSpec(memory_space=pl.ANY)],
        out_shape=jax.ShapeDtypeStruct((count, *rows.shape), rows.dtype),
        compiler_params=PARAMS,
        cost_estimate=cost(0, count * rows.size * 2),
        name="copies",
    )(rows, after)


def up_kernel(place_ref, own_ref, other_ref, gate_ref, up_ref, keep_ref, send_ref, weight_ref, acc_ref, sem_ref):
    core, half = place_ref[0], place_ref[1]
    steps, width = weight_ref.shape[1], weight_ref.shape[3]
    per, tokens = own_ref.shape[1] // steps, own_ref.shape[3]
    arrive = []
    for k in range(steps):
        for i, ref in enumerate((gate_ref, up_ref)):
            arrive.append(
                pltpu.make_async_copy(ref.at[:, pl.ds(k * width, width)], weight_ref.at[i, k], sem_ref.at[i, k])
            )
            arrive[-1].start()
    for k in range(steps):
        part = slice(k * per, (k + 1) * per)
        rows = jnp.concatenate(
            [zip_cores(core, own_ref[t, part], other_ref[t, part]) for t in range(2)], axis=1
        )
        for i in range(2):
            arrive[2 * k + i].wait()
            term = jnp.dot(weight_ref[i, k], rows, preferred_element_type=F32)
            if k == 0:
                acc_ref[i] = term
            else:
                acc_ref[i] += term
    for i in range(2):
        low, high = acc_ref[i, :, :tokens], acc_ref[i, :, tokens:]
        keep_ref[i] = jnp.where(half == 0, low, high)
        send_ref[i] = jnp.where(half == 0, high, low).astype(BF16)


def up_part(place, own, other, gate, up, steps=4):
    hidden, width = gate.shape
    rows, tokens = own.shape[-2:]
    own, other = (a.reshape(2, -1, rows, tokens) for a in (own, other))
    vmem = pl.BlockSpec(memory_space=pltpu.VMEM)
    hbm = pl.BlockSpec(memory_space=pltpu.HBM)
    return pl.pallas_call(
        up_kernel,
        in_specs=[pl.BlockSpec(memory_space=pltpu.SMEM), vmem, vmem, hbm, hbm],
        out_specs=[vmem, vmem],
        out_shape=[
            jax.ShapeDtypeStruct((2, hidden, tokens), F32),
            jax.ShapeDtypeStruct((2, hidden, tokens), BF16),
        ],
        scratch_shapes=[
            pltpu.VMEM((2, steps, hidden, width // steps), BF16),
            pltpu.VMEM((2, hidden, 2 * tokens), F32),
            pltpu.SemaphoreType.DMA((2, steps)),
        ],
        compiler_params=PARAMS,
        cost_estimate=cost(8 * hidden * width * tokens, 4 * hidden * width + 4 * own.size),
        name="gate_up",
    )(place, own, other, gate, up)


def down_kernel(place_ref, keep_ref, got_ref, near_ref, far_ref, hidden_ref, mine_ref, theirs_ref):
    side, step = pl.program_id(0), pl.program_id(1)
    core = place_ref[0]

    @pl.when((side == 0) & (step == 0))
    def _():
        preact, uppre = (keep_ref[i] + got_ref[i].astype(F32) for i in range(2))
        hidden_ref[...] = (preact / (1 + jnp.exp(-preact)) * uppre).astype(BF16)

    def part(ref):
        out = jnp.dot(ref[...], hidden_ref[...], preferred_element_type=F32).astype(BF16)
        count, rows, tokens = mine_ref.shape[1:]
        out = out.reshape(count, 2, rows, tokens)
        even, odd = out[:, 0], out[:, 1]
        mine_ref[0] = jnp.where(core == 0, even, odd)
        theirs_ref[0] = jnp.where(core == 0, odd, even)

    pl.when(side == 0)(lambda: part(near_ref))
    pl.when(side == 1)(lambda: part(far_ref))


def down_part(place, keep, got, near, far, rows, steps=2):
    width, hidden = near.shape
    tokens = keep.shape[-1]
    count = width // (2 * rows)
    whole = pl.BlockSpec((2, hidden, tokens), lambda s, k, _: (0, 0, 0))
    block = pl.BlockSpec(
        (1, count // steps, rows, tokens), lambda s, k, p: ((s + p[1]) % 2, k, 0, 0)
    )
    out = jax.ShapeDtypeStruct((2, count, rows, tokens), BF16)
    hidden_units, mine, theirs = pl.pallas_call(
        down_kernel,
        grid_spec=pltpu.PrefetchScalarGridSpec(
            num_scalar_prefetch=1,
            grid=(2, steps),
            in_specs=[
                whole,
                whole,
                pl.BlockSpec((width // steps, hidden), lambda s, k, _: (jnp.where(s == 0, k, steps - 1), 0)),
                pl.BlockSpec((width // steps, hidden), lambda s, k, _: (jnp.where(s == 1, k, 0), 0)),
            ],
            out_specs=[pl.BlockSpec((hidden, tokens), lambda s, k, _: (0, 0)), block, block],
        ),
        out_shape=[jax.ShapeDtypeStruct((hidden, tokens), BF16), out, out],
        compiler_params=PARAMS,
        cost_estimate=cost(0, 0),
        name="down",
    )(place, keep, got, near, far)
    return hidden_units, *(a.reshape(2 * count, rows, tokens) for a in (mine, theirs))


def student_kernel(gathered_ref, projector_ref, all_ref, out_ref):
    columns, count, rows, tokens = gathered_ref.shape
    rows = jnp.concatenate(
        [gathered_ref[:, i].reshape(columns * rows, tokens) for i in range(count)]
    )
    all_ref[...] = rows
    part = jnp.dot(projector_ref[...], rows, preferred_element_type=F32)

    @pl.when(pl.program_id(0) == 0)
    def _():
        out_ref[...] = part

    @pl.when(pl.program_id(0) != 0)
    def _():
        out_ref[...] += part


def student_part(gathered, projector, steps=8):
    columns, count, rows, tokens = gathered.shape
    mine, width = projector.shape
    return pl.pallas_call(
        student_kernel,
        grid=(steps,),
        in_specs=[
            pl.BlockSpec((columns, count // steps, rows, tokens), lambda k: (0, k, 0, 0)),
            pl.BlockSpec((mine, width // steps), lambda k: (0, k)),
        ],
        out_specs=[
            pl.BlockSpec((width // steps, tokens), lambda k: (k, 0)),
            pl.BlockSpec((mine, tokens), lambda k: (0, 0)),
        ],
        out_shape=[
            jax.ShapeDtypeStruct((width, tokens), BF16),
            jax.ShapeDtypeStruct((mine, tokens), F32),
        ],
        compiler_params=PARAMS,
        cost_estimate=cost(2 * mine * width * tokens, 4 * width * tokens + 2 * mine * width),
        name="student",
    )(gathered, projector)


def grad_kernel(terms_ref, student_out_ref, student_ref, residual_ref, grad_ref, rows_ref, sem_ref):
    steps, width = rows_ref.shape[:2]
    arrive = []
    for k in range(steps):
        arrive.append(
            pltpu.make_async_copy(student_ref.at[pl.ds(k * width, width)], rows_ref.at[k], sem_ref.at[k])
        )
        arrive[-1].start()
    teacher_out = jnp.sum(terms_ref[...].astype(F32), axis=0)
    residual = (student_out_ref[...] - teacher_out).astype(BF16)
    residual_ref[...] = residual
    for k in range(steps):
        arrive[k].wait()
        grad_ref[:, k * width : (k + 1) * width] = lax.dot_general(
            residual, rows_ref[k], (((1,), (1,)), ((), ())), preferred_element_type=F32
        ).astype(BF16)


def grad_part(terms, student_out, student_all, steps=8):
    rows, tokens = student_out.shape
    width = student_all.shape[0]
    vmem = pl.BlockSpec(memory_space=pltpu.VMEM)
    return pl.pallas_call(
        grad_kernel,
        in_specs=[vmem, vmem, pl.BlockSpec(memory_space=pltpu.HBM)],
        out_specs=[vmem, vmem],
        out_shape=[
            jax.ShapeDtypeStruct((rows, tokens), BF16),
            jax.ShapeDtypeStruct((rows, width), BF16),
        ],
        scratch_shapes=[
            pltpu.VMEM((steps, width // steps, tokens), BF16),
            pltpu.SemaphoreType.DMA((steps,)),
        ],
        compiler_params=PARAMS,
        cost_estimate=cost(2 * rows * width * tokens, 2 * (terms.size + width * tokens + rows * width)),
        name="gradient",
    )(terms, student_out, student_all)


def shards(teacher_rows, teacher_gate, teacher_up, teacher_down, student_rows, projector):
    place = jnp.stack([lax.axis_index(name) for name in ("core", "dp")]).astype(jnp.int32)
    rows = teacher_rows.shape[0]
    chips = lax.axis_size(CHIPS)
    across = lax.axis_size("y") // 2
    spread = functools.partial(lax.all_to_all, split_axis=0, concat_axis=0, tiled=True)

    trade = []
    for y in range(across):
        low, high = 2 * y, 2 * (y + across)
        trade += [(low, low), (low + 1, high), (high, low + 1), (high + 1, high + 1)]
    held = lax.ppermute(teacher_rows, ("y", "dp"), trade)
    quarter = teacher_down.shape[1] // 4
    far = [lax.ppermute(teacher_down[:, :quarter], "dp", SWAP)]
    held, far[0] = lax.optimization_barrier((held, far[0]))
    far.append(lax.ppermute(teacher_down[:, quarter:], "dp", SWAP))
    teacher_own = spread(copies(held, held, chips), CHIPS)
    student_part_rows = lax.all_gather(student_rows, ("y", "x"), axis=0)
    teacher_own, far[1], student_part_rows = lax.optimization_barrier(
        (teacher_own, far[1], student_part_rows)
    )
    teacher_other = lax.ppermute(teacher_own, "core", SWAP)
    student_gathered = lax.all_gather(student_part_rows, ("z", "core"), axis=0)

    keep, send = up_part(place, teacher_own, teacher_other, teacher_gate, teacher_up)
    got = lax.ppermute(send, "dp", SWAP)
    down_far = jnp.concatenate([part.T for part in far])
    teacher_hidden, mine, theirs = down_part(place, keep, got, teacher_down.T, down_far, rows)
    chip_sum = (
        mine.astype(F32) + lax.ppermute(theirs, "core", SWAP).astype(F32)
    ).astype(BF16)
    terms = spread(chip_sum, CHIPS)

    student_all, student_out = student_part(student_gathered, projector)
    residual_error, grad_local = grad_part(terms, student_out, student_all)
    grad_projector = grad_local + lax.ppermute(grad_local, "dp", SWAP)
    return (teacher_hidden, residual_error, grad_projector)


def solution(mesh):
    fine = Mesh(mesh.devices.reshape(8, 2, 8, 2, 2), (*CHIPS, "core", "dp"))
    blk = (*CHIPS, "core")
    return jax.shard_map(
        shards,
        mesh=fine,
        in_specs=(P(blk, "dp"),) * 5 + (P(blk, None),),
        out_specs=(P(blk, "dp"), P(blk, "dp"), P(blk, None)),
        check_vma=False,
    )
```

```python
import functools

import jax
import jax.numpy as jnp
from jax import lax
from jax.experimental import pallas as pl
from jax.experimental.pallas import tpu as pltpu
from jax.sharding import Mesh, PartitionSpec as P

CHIPS = ("y", "x", "z")
SWAP = [(0, 1), (1, 0)]
F32, BF16 = jnp.float32, jnp.bfloat16
PARAMS = pltpu.CompilerParams(vmem_limit_bytes=24 << 20)


def cost(flops, size):
    return pl.CostEstimate(flops=flops, bytes_accessed=size, transcendentals=0)


def zip_cores(core, own, other):
    count, rows, tokens = own.shape
    even = jnp.where(core == 0, own, other)
    odd = jnp.where(core == 0, other, own)
    return jnp.stack([even, odd], axis=1).reshape(count * 2 * rows, tokens)


def copies_kernel(rows_ref, _, out_ref):
    out_ref[...] = jnp.broadcast_to(rows_ref[...][None], out_ref.shape)


def copies(rows, after, count):
    return pl.pallas_call(
        copies_kernel,
        in_specs=[pl.BlockSpec(memory_space=pltpu.VMEM), pl.BlockSpec(memory_space=pl.ANY)],
        out_shape=jax.ShapeDtypeStruct((count, *rows.shape), rows.dtype),
        compiler_params=PARAMS,
        cost_estimate=cost(0, count * rows.size * 2),
        name="copies",
    )(rows, after)


def up_kernel(place_ref, own_ref, other_ref, gate_ref, up_ref, keep_ref, send_ref, weight_ref, acc_ref, sem_ref):
    core, half = place_ref[0], place_ref[1]
    steps, width = weight_ref.shape[1], weight_ref.shape[3]
    per, tokens = own_ref.shape[1] // steps, own_ref.shape[3]
    arrive = []
    for k in range(steps):
        for i, ref in enumerate((gate_ref, up_ref)):
            arrive.append(
                pltpu.make_async_copy(ref.at[:, pl.ds(k * width, width)], weight_ref.at[i, k], sem_ref.at[i, k])
            )
            arrive[-1].start()
    for k in range(steps):
        part = slice(k * per, (k + 1) * per)
        rows = jnp.concatenate(
            [zip_cores(core, own_ref[t, part], other_ref[t, part]) for t in range(2)], axis=1
        )
        for i in range(2):
            arrive[2 * k + i].wait()
            term = jnp.dot(weight_ref[i, k], rows, preferred_element_type=F32)
            if k == 0:
                acc_ref[i] = term
            else:
                acc_ref[i] += term
    for i in range(2):
        low, high = acc_ref[i, :, :tokens], acc_ref[i, :, tokens:]
        keep_ref[i] = jnp.where(half == 0, low, high)
        send_ref[i] = jnp.where(half == 0, high, low).astype(BF16)


def up_part(place, own, other, gate, up, steps=4):
    hidden, width = gate.shape
    rows, tokens = own.shape[-2:]
    own, other = (a.reshape(2, -1, rows, tokens) for a in (own, other))
    vmem = pl.BlockSpec(memory_space=pltpu.VMEM)
    hbm = pl.BlockSpec(memory_space=pltpu.HBM)
    return pl.pallas_call(
        up_kernel,
        in_specs=[pl.BlockSpec(memory_space=pltpu.SMEM), vmem, vmem, hbm, hbm],
        out_specs=[vmem, vmem],
        out_shape=[
            jax.ShapeDtypeStruct((2, hidden, tokens), F32),
            jax.ShapeDtypeStruct((2, hidden, tokens), BF16),
        ],
        scratch_shapes=[
            pltpu.VMEM((2, steps, hidden, width // steps), BF16),
            pltpu.VMEM((2, hidden, 2 * tokens), F32),
            pltpu.SemaphoreType.DMA((2, steps)),
        ],
        compiler_params=PARAMS,
        cost_estimate=cost(8 * hidden * width * tokens, 4 * hidden * width + 4 * own.size),
        name="gate_up",
    )(place, own, other, gate, up)


def down_kernel(place_ref, keep_ref, got_ref, near_ref, far_ref, hidden_ref, mine_ref, theirs_ref):
    side, step = pl.program_id(0), pl.program_id(1)
    core = place_ref[0]

    @pl.when((side == 0) & (step == 0))
    def _():
        preact, uppre = (keep_ref[i] + got_ref[i].astype(F32) for i in range(2))
        hidden_ref[...] = (preact / (1 + jnp.exp(-preact)) * uppre).astype(BF16)

    def part(ref):
        out = jnp.dot(ref[...], hidden_ref[...], preferred_element_type=F32).astype(BF16)
        count, rows, tokens = mine_ref.shape[1:]
        out = out.reshape(count, 2, rows, tokens)
        even, odd = out[:, 0], out[:, 1]
        mine_ref[0] = jnp.where(core == 0, even, odd)
        theirs_ref[0] = jnp.where(core == 0, odd, even)

    pl.when(side == 0)(lambda: part(near_ref))
    pl.when(side == 1)(lambda: part(far_ref))


def down_part(place, keep, got, near, far, rows, steps=2):
    width, hidden = near.shape
    tokens = keep.shape[-1]
    count = width // (2 * rows)
    whole = pl.BlockSpec((2, hidden, tokens), lambda s, k, _: (0, 0, 0))
    block = pl.BlockSpec(
        (1, count // steps, rows, tokens), lambda s, k, p: ((s + p[1]) % 2, k, 0, 0)
    )
    out = jax.ShapeDtypeStruct((2, count, rows, tokens), BF16)
    hidden_units, mine, theirs = pl.pallas_call(
        down_kernel,
        grid_spec=pltpu.PrefetchScalarGridSpec(
            num_scalar_prefetch=1,
            grid=(2, steps),
            in_specs=[
                whole,
                whole,
                pl.BlockSpec((width // steps, hidden), lambda s, k, _: (jnp.where(s == 0, k, steps - 1), 0)),
                pl.BlockSpec((width // steps, hidden), lambda s, k, _: (jnp.where(s == 1, k, 0), 0)),
            ],
            out_specs=[pl.BlockSpec((hidden, tokens), lambda s, k, _: (0, 0)), block, block],
        ),
        out_shape=[jax.ShapeDtypeStruct((hidden, tokens), BF16), out, out],
        compiler_params=PARAMS,
        cost_estimate=cost(0, 0),
        name="down",
    )(place, keep, got, near, far)
    return hidden_units, *(a.reshape(2 * count, rows, tokens) for a in (mine, theirs))


def student_kernel(place_ref, gathered_ref, projector_ref, all_ref, out_ref):
    columns, _, rows, tokens = gathered_ref.shape
    low, high = (gathered_ref[:, i].reshape(columns * rows, tokens) for i in range(2))
    even = place_ref[2] == 0
    rows = jnp.concatenate([jnp.where(even, low, high), jnp.where(even, high, low)])
    all_ref[...] = rows
    part = jnp.dot(projector_ref[...], rows, preferred_element_type=F32)

    @pl.when(pl.program_id(0) == 0)
    def _():
        out_ref[...] = part

    @pl.when(pl.program_id(0) != 0)
    def _():
        out_ref[...] += part


def student_part(place, gathered, projector):
    columns, count, rows, tokens = gathered.shape
    mine, width = projector.shape
    steps = count // 2
    return pl.pallas_call(
        student_kernel,
        grid_spec=pltpu.PrefetchScalarGridSpec(
            num_scalar_prefetch=1,
            grid=(steps,),
            in_specs=[
                pl.BlockSpec((columns, 2, rows, tokens), lambda k, p: (0, k ^ p[3], 0, 0)),
                pl.BlockSpec((mine, width // steps), lambda k, _: (0, k)),
            ],
            out_specs=[
                pl.BlockSpec((width // steps, tokens), lambda k, _: (k, 0)),
                pl.BlockSpec((mine, tokens), lambda k, _: (0, 0)),
            ],
        ),
        out_shape=[
            jax.ShapeDtypeStruct((width, tokens), BF16),
            jax.ShapeDtypeStruct((mine, tokens), F32),
        ],
        compiler_params=PARAMS,
        cost_estimate=cost(2 * mine * width * tokens, 4 * width * tokens + 2 * mine * width),
        name="student",
    )(place, gathered, projector)


def grad_kernel(terms_ref, student_out_ref, student_ref, residual_ref, grad_ref, rows_ref, sem_ref):
    steps, width = rows_ref.shape[:2]
    arrive = []
    for k in range(steps):
        arrive.append(
            pltpu.make_async_copy(student_ref.at[pl.ds(k * width, width)], rows_ref.at[k], sem_ref.at[k])
        )
        arrive[-1].start()
    teacher_out = jnp.sum(terms_ref[...].astype(F32), axis=0)
    residual = (student_out_ref[...] - teacher_out).astype(BF16)
    residual_ref[...] = residual
    for k in range(steps):
        arrive[k].wait()
        grad_ref[:, k * width : (k + 1) * width] = lax.dot_general(
            residual, rows_ref[k], (((1,), (1,)), ((), ())), preferred_element_type=F32
        ).astype(BF16)


def grad_part(terms, student_out, student_all, steps=8):
    rows, tokens = student_out.shape
    width = student_all.shape[0]
    vmem = pl.BlockSpec(memory_space=pltpu.VMEM)
    return pl.pallas_call(
        grad_kernel,
        in_specs=[vmem, vmem, pl.BlockSpec(memory_space=pltpu.HBM)],
        out_specs=[vmem, vmem],
        out_shape=[
            jax.ShapeDtypeStruct((rows, tokens), BF16),
            jax.ShapeDtypeStruct((rows, width), BF16),
        ],
        scratch_shapes=[
            pltpu.VMEM((steps, width // steps, tokens), BF16),
            pltpu.SemaphoreType.DMA((steps,)),
        ],
        compiler_params=PARAMS,
        cost_estimate=cost(2 * rows * width * tokens, 2 * (terms.size + width * tokens + rows * width)),
        name="gradient",
    )(terms, student_out, student_all)


def shards(teacher_rows, teacher_gate, teacher_up, teacher_down, student_rows, projector):
    place = jnp.stack([lax.axis_index(name) for name in ("core", "dp", "x", "y")]).astype(jnp.int32)
    rows = teacher_rows.shape[0]
    chips = lax.axis_size(CHIPS)
    across = lax.axis_size("y") // 2
    spread = functools.partial(lax.all_to_all, split_axis=0, concat_axis=0, tiled=True)

    trade = []
    for y in range(across):
        low, high = 2 * y, 2 * (y + across)
        trade += [(low, low), (low + 1, high), (high, low + 1), (high + 1, high + 1)]
    held = lax.ppermute(teacher_rows, ("y", "dp"), trade)
    down_far = lax.ppermute(teacher_down, "dp", SWAP)
    teacher_own = spread(copies(held, held, chips), CHIPS)
    column = student_rows[None]
    for name in ("x", "y"):
        bit, size = 1, lax.axis_size(name)
        while bit < size:
            moved = lax.ppermute(column, name, [(i, i ^ bit) for i in range(size)])
            column = jnp.concatenate([column, moved])
            bit *= 2
    teacher_own, down_far, column = lax.optimization_barrier(
        (teacher_own, down_far, column)
    )
    teacher_other = lax.ppermute(teacher_own, "core", SWAP)
    student_gathered = lax.all_gather(column, ("z", "core"), axis=0)

    keep, send = up_part(place, teacher_own, teacher_other, teacher_gate, teacher_up)
    got = lax.ppermute(send, "dp", SWAP)
    teacher_hidden, mine, theirs = down_part(place, keep, got, teacher_down.T, down_far.T, rows)
    chip_sum = (
        mine.astype(F32) + lax.ppermute(theirs, "core", SWAP).astype(F32)
    ).astype(BF16)
    terms = spread(chip_sum, CHIPS)

    student_all, student_out = student_part(place, student_gathered, projector)
    residual_error, grad_local = grad_part(terms, student_out, student_all)
    grad_projector = grad_local + lax.ppermute(grad_local, "dp", SWAP)
    return (teacher_hidden, residual_error, grad_projector)


def solution(mesh):
    fine = Mesh(mesh.devices.reshape(8, 2, 8, 2, 2), (*CHIPS, "core", "dp"))
    blk = (*CHIPS, "core")
    return jax.shard_map(
        shards,
        mesh=fine,
        in_specs=(P(blk, "dp"),) * 5 + (P(blk, None),),
        out_specs=(P(blk, "dp"), P(blk, "dp"), P(blk, None)),
        check_vma=False,
    )
```

```python
import functools

import jax
import jax.numpy as jnp
from jax import lax
from jax.experimental import pallas as pl
from jax.experimental.pallas import tpu as pltpu
from jax.sharding import Mesh, PartitionSpec as P

CHIPS = ("y", "x", "z")
SWAP = [(0, 1), (1, 0)]
F32, BF16 = jnp.float32, jnp.bfloat16
PARAMS = pltpu.CompilerParams(vmem_limit_bytes=24 << 20)


def cost(flops, size):
    return pl.CostEstimate(flops=flops, bytes_accessed=size, transcendentals=0)


def zip_cores(core, own, other):
    count, rows, tokens = own.shape
    even = jnp.where(core == 0, own, other)
    odd = jnp.where(core == 0, other, own)
    return jnp.stack([even, odd], axis=1).reshape(count * 2 * rows, tokens)


def copies_kernel(rows_ref, _, out_ref):
    out_ref[...] = jnp.broadcast_to(rows_ref[...][None], out_ref.shape)


def copies(rows, after, count):
    return pl.pallas_call(
        copies_kernel,
        in_specs=[pl.BlockSpec(memory_space=pltpu.VMEM), pl.BlockSpec(memory_space=pl.ANY)],
        out_shape=jax.ShapeDtypeStruct((count, *rows.shape), rows.dtype),
        compiler_params=PARAMS,
        cost_estimate=cost(0, count * rows.size * 2),
        name="copies",
    )(rows, after)


def pack_kernel(gate_ref, up_ref, out_ref):
    out_ref[0] = gate_ref[...]
    out_ref[1] = up_ref[...]


def pack(gate, up, steps=4):
    hidden, width = gate.shape
    block = pl.BlockSpec((hidden, width // steps), lambda k: (0, k))
    return pl.pallas_call(
        pack_kernel,
        grid=(steps,),
        in_specs=[block, block],
        out_specs=pl.BlockSpec((2, hidden, width // steps), lambda k: (0, 0, k)),
        out_shape=jax.ShapeDtypeStruct((2, hidden, width), BF16),
        compiler_params=PARAMS,
        cost_estimate=cost(0, 8 * hidden * width),
        name="pack",
    )(gate, up)


def up_kernel(place_ref, own_ref, other_ref, weight_ref, keep_ref, send_ref, acc_ref):
    step, last = pl.program_id(0), pl.num_programs(0) - 1
    core, half = place_ref[0], place_ref[1]
    tokens = own_ref.shape[-1]
    rows = jnp.concatenate(
        [zip_cores(core, own_ref[t], other_ref[t]) for t in range(2)], axis=1
    )
    for i in range(2):
        term = jnp.dot(weight_ref[i], rows, preferred_element_type=F32)

        @pl.when(step == 0)
        def _():
            acc_ref[i] = term

        @pl.when(step != 0)
        def _():
            acc_ref[i] += term

    @pl.when(step == last)
    def _():
        for i in range(2):
            low, high = acc_ref[i, :, :tokens], acc_ref[i, :, tokens:]
            keep_ref[i] = jnp.where(half == 0, low, high)
            send_ref[i] = jnp.where(half == 0, high, low).astype(BF16)


def up_part(place, own, other, weights, steps=4):
    hidden, width = weights.shape[1:]
    rows, tokens = own.shape[-2:]
    per = width // (2 * rows * steps)
    own, other = (a.reshape(2, -1, rows, tokens) for a in (own, other))
    block = pl.BlockSpec((2, per, rows, tokens), lambda k, _: (0, k, 0, 0))
    whole = pl.BlockSpec((2, hidden, tokens), lambda k, _: (0, 0, 0))
    return pl.pallas_call(
        up_kernel,
        grid_spec=pltpu.PrefetchScalarGridSpec(
            num_scalar_prefetch=1,
            grid=(steps,),
            in_specs=[
                block,
                block,
                pl.BlockSpec((2, hidden, width // steps), lambda k, _: (0, 0, k)),
            ],
            out_specs=[whole, whole],
            scratch_shapes=[pltpu.VMEM((2, hidden, 2 * tokens), F32)],
        ),
        out_shape=[
            jax.ShapeDtypeStruct((2, hidden, tokens), F32),
            jax.ShapeDtypeStruct((2, hidden, tokens), BF16),
        ],
        compiler_params=PARAMS,
        cost_estimate=cost(8 * hidden * width * tokens, 4 * hidden * width + 4 * own.size),
        name="gate_up",
    )(place, own, other, weights)


def down_kernel(place_ref, keep_ref, got_ref, near_ref, far_ref, hidden_ref, mine_ref, theirs_ref):
    side, step = pl.program_id(0), pl.program_id(1)
    core = place_ref[0]

    @pl.when((side == 0) & (step == 0))
    def _():
        preact, uppre = (keep_ref[i] + got_ref[i].astype(F32) for i in range(2))
        hidden_ref[...] = (preact / (1 + jnp.exp(-preact)) * uppre).astype(BF16)

    def part(ref):
        out = jnp.dot(ref[...], hidden_ref[...], preferred_element_type=F32).astype(BF16)
        count, rows, tokens = mine_ref.shape[1:]
        out = out.reshape(count, 2, rows, tokens)
        even, odd = out[:, 0], out[:, 1]
        mine_ref[0] = jnp.where(core == 0, even, odd)
        theirs_ref[0] = jnp.where(core == 0, odd, even)

    pl.when(side == 0)(lambda: part(near_ref))
    pl.when(side == 1)(lambda: part(far_ref))


def down_part(place, keep, got, near, far, rows, steps=2):
    width, hidden = near.shape
    tokens = keep.shape[-1]
    count = width // (2 * rows)
    whole = pl.BlockSpec((2, hidden, tokens), lambda s, k, _: (0, 0, 0))
    block = pl.BlockSpec(
        (1, count // steps, rows, tokens), lambda s, k, p: ((s + p[1]) % 2, k, 0, 0)
    )
    out = jax.ShapeDtypeStruct((2, count, rows, tokens), BF16)
    hidden_units, mine, theirs = pl.pallas_call(
        down_kernel,
        grid_spec=pltpu.PrefetchScalarGridSpec(
            num_scalar_prefetch=1,
            grid=(2, steps),
            in_specs=[
                whole,
                whole,
                pl.BlockSpec((width // steps, hidden), lambda s, k, _: (jnp.where(s == 0, k, steps - 1), 0)),
                pl.BlockSpec((width // steps, hidden), lambda s, k, _: (jnp.where(s == 1, k, 0), 0)),
            ],
            out_specs=[pl.BlockSpec((hidden, tokens), lambda s, k, _: (0, 0)), block, block],
        ),
        out_shape=[jax.ShapeDtypeStruct((hidden, tokens), BF16), out, out],
        compiler_params=PARAMS,
        cost_estimate=cost(0, 0),
        name="down",
    )(place, keep, got, near, far)
    return hidden_units, *(a.reshape(2 * count, rows, tokens) for a in (mine, theirs))


def student_kernel(place_ref, own_ref, other_ref, projector_ref, out_ref):
    rows = zip_cores(place_ref[0], own_ref[...], other_ref[...])
    part = jnp.dot(projector_ref[...], rows, preferred_element_type=F32)

    @pl.when(pl.program_id(0) == 0)
    def _():
        out_ref[...] = part

    @pl.when(pl.program_id(0) != 0)
    def _():
        out_ref[...] += part


def student_part(place, own, other, projector, steps=4):
    count, rows, tokens = own.shape
    mine, width = projector.shape
    block = pl.BlockSpec((count // steps, rows, tokens), lambda k, _: (k, 0, 0))
    return pl.pallas_call(
        student_kernel,
        grid_spec=pltpu.PrefetchScalarGridSpec(
            num_scalar_prefetch=1,
            grid=(steps,),
            in_specs=[block, block, pl.BlockSpec((mine, width // steps), lambda k, _: (0, k))],
            out_specs=pl.BlockSpec((mine, tokens), lambda k, _: (0, 0)),
        ),
        out_shape=jax.ShapeDtypeStruct((mine, tokens), F32),
        compiler_params=PARAMS,
        cost_estimate=cost(2 * mine * width * tokens, 2 * width * tokens + 2 * mine * width),
        name="student",
    )(place, own, other, projector)


def grad_kernel(place_ref, terms_ref, student_out_ref, own_ref, other_ref, residual_ref, grad_ref):
    @pl.when(pl.program_id(0) == 0)
    def _():
        teacher_out = jnp.sum(terms_ref[...].astype(F32), axis=0)
        residual_ref[...] = (student_out_ref[...] - teacher_out).astype(BF16)

    rows = zip_cores(place_ref[0], own_ref[...], other_ref[...])
    grad_ref[...] = lax.dot_general(
        residual_ref[...], rows, (((1,), (1,)), ((), ())), preferred_element_type=F32
    ).astype(BF16)


def grad_part(place, terms, student_out, own, other, steps=4):
    mine, tokens = student_out.shape
    count, rows = own.shape[:2]
    width = 2 * count * rows
    small = pl.BlockSpec((mine, tokens), lambda k, _: (0, 0))
    block = pl.BlockSpec((count // steps, rows, tokens), lambda k, _: (k, 0, 0))
    return pl.pallas_call(
        grad_kernel,
        grid_spec=pltpu.PrefetchScalarGridSpec(
            num_scalar_prefetch=1,
            grid=(steps,),
            in_specs=[pl.BlockSpec(terms.shape, lambda k, _: (0, 0, 0)), small, block, block],
            out_specs=[small, pl.BlockSpec((mine, width // steps), lambda k, _: (0, k))],
        ),
        out_shape=[
            jax.ShapeDtypeStruct((mine, tokens), BF16),
            jax.ShapeDtypeStruct((mine, width), BF16),
        ],
        compiler_params=PARAMS,
        cost_estimate=cost(2 * mine * width * tokens, 2 * (terms.size + width * tokens + mine * width)),
        name="gradient",
    )(place, terms, student_out, own, other)


def shards(teacher_rows, teacher_gate, teacher_up, teacher_down, student_rows, projector):
    place = jnp.stack([lax.axis_index(name) for name in ("core", "dp")]).astype(jnp.int32)
    rows = teacher_rows.shape[0]
    chips = lax.axis_size(CHIPS)
    across = lax.axis_size("y") // 2
    spread = functools.partial(lax.all_to_all, split_axis=0, concat_axis=0, tiled=True)

    trade = []
    for y in range(across):
        low, high = 2 * y, 2 * (y + across)
        trade += [(low, low), (low + 1, high), (high, low + 1), (high + 1, high + 1)]
    held = lax.ppermute(teacher_rows, ("y", "dp"), trade)
    down_far = lax.ppermute(teacher_down, "dp", SWAP)
    teacher_own = spread(copies(held, held, chips), CHIPS)
    teacher_own, down_far, down_near, student_copies, gate_and_up = lax.optimization_barrier(
        (
            teacher_own,
            down_far,
            teacher_down.T,
            copies(student_rows, held, chips),
            pack(teacher_gate, teacher_up),
        )
    )
    teacher_other = lax.ppermute(teacher_own, "core", SWAP)
    student_own = spread(student_copies, CHIPS)

    keep, send = up_part(place, teacher_own, teacher_other, gate_and_up)
    send, down_far = lax.optimization_barrier((send, down_far))
    got = lax.ppermute(send, "dp", SWAP)
    teacher_hidden, mine, theirs = down_part(place, keep, got, down_near, down_far.T, rows)
    chip_sum = (
        mine.astype(F32) + lax.ppermute(theirs, "core", SWAP).astype(F32)
    ).astype(BF16)
    terms = spread(chip_sum, CHIPS)

    student_other = lax.ppermute(student_own, "core", SWAP)
    student_out = student_part(place, student_own, student_other, projector)
    residual_error, grad_local = grad_part(place, terms, student_out, student_own, student_other)
    grad_projector = grad_local + lax.ppermute(grad_local, "dp", SWAP)
    return (teacher_hidden, residual_error, grad_projector)


def solution(mesh):
    fine = Mesh(mesh.devices.reshape(8, 2, 8, 2, 2), (*CHIPS, "core", "dp"))
    blk = (*CHIPS, "core")
    return jax.shard_map(
        shards,
        mesh=fine,
        in_specs=(P(blk, "dp"),) * 5 + (P(blk, None),),
        out_specs=(P(blk, "dp"), P(blk, "dp"), P(blk, None)),
        check_vma=False,
    )
```

```python
import functools

import jax
import jax.numpy as jnp
from jax import lax
from jax.experimental import pallas as pl
from jax.experimental.pallas import tpu as pltpu
from jax.sharding import Mesh, PartitionSpec as P

CHIPS = ("y", "x", "z")
SWAP = [(0, 1), (1, 0)]
F32, BF16 = jnp.float32, jnp.bfloat16
PARAMS = pltpu.CompilerParams(vmem_limit_bytes=24 << 20)


def cost(flops, size):
    return pl.CostEstimate(flops=flops, bytes_accessed=size, transcendentals=0)


def zip_cores(core, own, other):
    count, rows, tokens = own.shape
    even = jnp.where(core == 0, own, other)
    odd = jnp.where(core == 0, other, own)
    return jnp.stack([even, odd], axis=1).reshape(count * 2 * rows, tokens)


def copies_kernel(teacher_ref, student_ref, out_ref):
    rows = teacher_ref.shape[0]
    shape = (out_ref.shape[0], *teacher_ref.shape)
    out_ref[:, :rows] = jnp.broadcast_to(teacher_ref[...][None], shape)
    out_ref[:, rows:] = jnp.broadcast_to(student_ref[...][None], shape)


def copies(teacher, student, count):
    rows, tokens = teacher.shape
    return pl.pallas_call(
        copies_kernel,
        out_shape=jax.ShapeDtypeStruct((count, 2 * rows, tokens), BF16),
        compiler_params=PARAMS,
        cost_estimate=cost(0, 4 * count * rows * tokens),
        name="copies",
    )(teacher, student)


def pack_kernel(gate_ref, up_ref, out_ref):
    out_ref[0] = gate_ref[...]
    out_ref[1] = up_ref[...]


def pack(gate, up, steps=4):
    hidden, width = gate.shape
    block = pl.BlockSpec((hidden, width // steps), lambda k: (0, k))
    return pl.pallas_call(
        pack_kernel,
        grid=(steps,),
        in_specs=[block, block],
        out_specs=pl.BlockSpec((2, hidden, width // steps), lambda k: (0, 0, k)),
        out_shape=jax.ShapeDtypeStruct((2, hidden, width), BF16),
        compiler_params=PARAMS,
        cost_estimate=cost(0, 8 * hidden * width),
        name="pack",
    )(gate, up)


def up_kernel(steps, place_ref, own_ref, other_ref, weight_ref, keep_ref, send_ref, acc_ref):
    core, half = place_ref[0], place_ref[1]
    count, tokens = own_ref.shape[1], own_ref.shape[3]
    rows, width = own_ref.shape[2] // 2, weight_ref.shape[2]
    for k in range(steps):
        part = slice(k * count // steps, (k + 1) * count // steps)
        columns = slice(k * width // steps, (k + 1) * width // steps)
        block = jnp.concatenate(
            [zip_cores(core, own_ref[t, part, :rows], other_ref[t, part, :rows]) for t in range(2)],
            axis=1,
        )
        for i in range(2):
            term = jnp.dot(weight_ref[i, :, columns], block, preferred_element_type=F32)
            if k == 0:
                acc_ref[i] = term
            else:
                acc_ref[i] += term
    for i in range(2):
        low, high = acc_ref[i, :, :tokens], acc_ref[i, :, tokens:]
        keep_ref[i] = jnp.where(half == 0, low, high)
        send_ref[i] = jnp.where(half == 0, high, low).astype(BF16)


def up_part(place, own, other, weights, steps=4):
    hidden, width = weights.shape[1:]
    tokens = own.shape[-1]
    own, other = (a.reshape(2, -1, *a.shape[1:]) for a in (own, other))
    vmem = pl.BlockSpec(memory_space=pltpu.VMEM)
    return pl.pallas_call(
        functools.partial(up_kernel, steps),
        in_specs=[pl.BlockSpec(memory_space=pltpu.SMEM), vmem, vmem, vmem],
        out_specs=[vmem, vmem],
        out_shape=[
            jax.ShapeDtypeStruct((2, hidden, tokens), F32),
            jax.ShapeDtypeStruct((2, hidden, tokens), BF16),
        ],
        scratch_shapes=[pltpu.VMEM((2, hidden, 2 * tokens), F32)],
        compiler_params=PARAMS,
        cost_estimate=cost(8 * hidden * width * tokens, 4 * hidden * width + 4 * own.size),
        name="gate_up",
    )(place, own, other, weights)


def down_kernel(place_ref, keep_ref, got_ref, near_ref, far_ref, hidden_ref, mine_ref, theirs_ref):
    side, step = pl.program_id(0), pl.program_id(1)
    core = place_ref[0]

    @pl.when((side == 0) & (step == 0))
    def _():
        preact, uppre = (keep_ref[i] + got_ref[i].astype(F32) for i in range(2))
        hidden_ref[...] = (preact / (1 + jnp.exp(-preact)) * uppre).astype(BF16)

    def part(ref):
        out = jnp.dot(ref[...], hidden_ref[...], preferred_element_type=F32).astype(BF16)
        count, rows, tokens = mine_ref.shape[1:]
        out = out.reshape(count, 2, rows, tokens)
        even, odd = out[:, 0], out[:, 1]
        mine_ref[0] = jnp.where(core == 0, even, odd)
        theirs_ref[0] = jnp.where(core == 0, odd, even)

    pl.when(side == 0)(lambda: part(near_ref))
    pl.when(side == 1)(lambda: part(far_ref))


def down_part(place, keep, got, near, far, rows, steps=2):
    width, hidden = near.shape
    tokens = keep.shape[-1]
    count = width // (2 * rows)
    whole = pl.BlockSpec((2, hidden, tokens), lambda s, k, _: (0, 0, 0))
    block = pl.BlockSpec(
        (1, count // steps, rows, tokens), lambda s, k, p: ((s + p[1]) % 2, k, 0, 0)
    )
    out = jax.ShapeDtypeStruct((2, count, rows, tokens), BF16)
    hidden_units, mine, theirs = pl.pallas_call(
        down_kernel,
        grid_spec=pltpu.PrefetchScalarGridSpec(
            num_scalar_prefetch=1,
            grid=(2, steps),
            in_specs=[
                whole,
                whole,
                pl.BlockSpec((width // steps, hidden), lambda s, k, _: (jnp.where(s == 0, k, steps - 1), 0)),
                pl.BlockSpec((width // steps, hidden), lambda s, k, _: (jnp.where(s == 1, k, 0), 0)),
            ],
            out_specs=[pl.BlockSpec((hidden, tokens), lambda s, k, _: (0, 0)), block, block],
        ),
        out_shape=[jax.ShapeDtypeStruct((hidden, tokens), BF16), out, out],
        compiler_params=PARAMS,
        cost_estimate=cost(0, 0),
        name="down",
    )(place, keep, got, near, far)
    return hidden_units, *(a.reshape(2 * count, rows, tokens) for a in (mine, theirs))


def student_kernel(place_ref, own_ref, other_ref, projector_ref, out_ref):
    rows = zip_cores(place_ref[0], own_ref[...], other_ref[...])
    part = jnp.dot(projector_ref[...], rows, preferred_element_type=F32)

    @pl.when(pl.program_id(0) == 0)
    def _():
        out_ref[...] = part

    @pl.when(pl.program_id(0) != 0)
    def _():
        out_ref[...] += part


def student_part(place, own, other, projector, steps=4):
    count, rows, tokens = own.shape
    mine, width = projector.shape
    block = pl.BlockSpec((count // steps, rows // 2, tokens), lambda k, _: (k, 1, 0))
    return pl.pallas_call(
        student_kernel,
        grid_spec=pltpu.PrefetchScalarGridSpec(
            num_scalar_prefetch=1,
            grid=(steps,),
            in_specs=[block, block, pl.BlockSpec((mine, width // steps), lambda k, _: (0, k))],
            out_specs=pl.BlockSpec((mine, tokens), lambda k, _: (0, 0)),
        ),
        out_shape=jax.ShapeDtypeStruct((mine, tokens), F32),
        compiler_params=PARAMS,
        cost_estimate=cost(2 * mine * width * tokens, 2 * width * tokens + 2 * mine * width),
        name="student",
    )(place, own, other, projector)


def grad_kernel(place_ref, terms_ref, student_out_ref, own_ref, other_ref, residual_ref, grad_ref):
    @pl.when(pl.program_id(0) == 0)
    def _():
        teacher_out = jnp.sum(terms_ref[...].astype(F32), axis=0)
        residual_ref[...] = (student_out_ref[...] - teacher_out).astype(BF16)

    rows = zip_cores(place_ref[0], own_ref[...], other_ref[...])
    grad_ref[...] = lax.dot_general(
        residual_ref[...], rows, (((1,), (1,)), ((), ())), preferred_element_type=F32
    ).astype(BF16)


def grad_part(place, terms, student_out, own, other, steps=4):
    mine, tokens = student_out.shape
    count, rows = own.shape[:2]
    width = count * rows
    small = pl.BlockSpec((mine, tokens), lambda k, _: (0, 0))
    block = pl.BlockSpec((count // steps, rows // 2, tokens), lambda k, _: (k, 1, 0))
    return pl.pallas_call(
        grad_kernel,
        grid_spec=pltpu.PrefetchScalarGridSpec(
            num_scalar_prefetch=1,
            grid=(steps,),
            in_specs=[pl.BlockSpec(terms.shape, lambda k, _: (0, 0, 0)), small, block, block],
            out_specs=[small, pl.BlockSpec((mine, width // steps), lambda k, _: (0, k))],
        ),
        out_shape=[
            jax.ShapeDtypeStruct((mine, tokens), BF16),
            jax.ShapeDtypeStruct((mine, width), BF16),
        ],
        compiler_params=PARAMS,
        cost_estimate=cost(2 * mine * width * tokens, 2 * (terms.size + width * tokens + mine * width)),
        name="gradient",
    )(place, terms, student_out, own, other)


def shards(teacher_rows, teacher_gate, teacher_up, teacher_down, student_rows, projector):
    place = jnp.stack([lax.axis_index(name) for name in ("core", "dp")]).astype(jnp.int32)
    rows = teacher_rows.shape[0]
    chips = lax.axis_size(CHIPS)
    across = lax.axis_size("y") // 2
    spread = functools.partial(lax.all_to_all, split_axis=0, concat_axis=0, tiled=True)

    trade = []
    for y in range(across):
        low, high = 2 * y, 2 * (y + across)
        trade += [(low, low), (low + 1, high), (high, low + 1), (high + 1, high + 1)]
    held = lax.ppermute(teacher_rows, ("y", "dp"), trade)
    down_far = lax.ppermute(teacher_down, "dp", SWAP)
    own = spread(copies(held, student_rows, chips), CHIPS)
    own, down_far, down_near, gate_and_up = lax.optimization_barrier(
        (own, down_far, teacher_down.T, pack(teacher_gate, teacher_up))
    )
    other = lax.ppermute(own, "core", SWAP)

    keep, send = up_part(place, own, other, gate_and_up)
    send, down_far = lax.optimization_barrier((send, down_far))
    got = lax.ppermute(send, "dp", SWAP)
    teacher_hidden, mine, theirs = down_part(place, keep, got, down_near, down_far.T, rows)
    chip_sum = (
        mine.astype(F32) + lax.ppermute(theirs, "core", SWAP).astype(F32)
    ).astype(BF16)
    terms = spread(chip_sum, CHIPS)

    student_out = student_part(place, own, other, projector)
    residual_error, grad_local = grad_part(place, terms, student_out, own, other)
    grad_projector = grad_local + lax.ppermute(grad_local, "dp", SWAP)
    return (teacher_hidden, residual_error, grad_projector)


def solution(mesh):
    fine = Mesh(mesh.devices.reshape(8, 2, 8, 2, 2), (*CHIPS, "core", "dp"))
    blk = (*CHIPS, "core")
    return jax.shard_map(
        shards,
        mesh=fine,
        in_specs=(P(blk, "dp"),) * 5 + (P(blk, None),),
        out_specs=(P(blk, "dp"), P(blk, "dp"), P(blk, None)),
        check_vma=False,
    )
```

```python
import functools

import jax
import jax.numpy as jnp
from jax import lax
from jax.experimental import pallas as pl
from jax.experimental.pallas import tpu as pltpu
from jax.sharding import Mesh, PartitionSpec as P

CHIPS = ("y", "x", "z")
SWAP = [(0, 1), (1, 0)]
F32, BF16 = jnp.float32, jnp.bfloat16
PARAMS = pltpu.CompilerParams(vmem_limit_bytes=24 << 20)


def cost(flops, size):
    return pl.CostEstimate(flops=flops, bytes_accessed=size, transcendentals=0)


def zip_cores(core, own, other):
    count, rows, tokens = own.shape
    even = jnp.where(core == 0, own, other)
    odd = jnp.where(core == 0, other, own)
    return jnp.stack([even, odd], axis=1).reshape(count * 2 * rows, tokens)


def copies_kernel(rows_ref, _, out_ref):
    out_ref[...] = jnp.broadcast_to(rows_ref[...][None], out_ref.shape)


def copies(rows, after, count):
    return pl.pallas_call(
        copies_kernel,
        in_specs=[pl.BlockSpec(memory_space=pltpu.VMEM), pl.BlockSpec(memory_space=pl.ANY)],
        out_shape=jax.ShapeDtypeStruct((count, *rows.shape), rows.dtype),
        compiler_params=PARAMS,
        cost_estimate=cost(0, count * rows.size * 2),
        name="copies",
    )(rows, after)


def pack_kernel(gate_ref, up_ref, out_ref):
    out_ref[0] = gate_ref[...]
    out_ref[1] = up_ref[...]


def pack(gate, up, steps=4):
    hidden, width = gate.shape
    block = pl.BlockSpec((hidden, width // steps), lambda k: (0, k))
    return pl.pallas_call(
        pack_kernel,
        grid=(steps,),
        in_specs=[block, block],
        out_specs=pl.BlockSpec((2, hidden, width // steps), lambda k: (0, 0, k)),
        out_shape=jax.ShapeDtypeStruct((2, hidden, width), BF16),
        compiler_params=PARAMS,
        cost_estimate=cost(0, 8 * hidden * width),
        name="pack",
    )(gate, up)


def up_kernel(steps, place_ref, own_ref, other_ref, weight_ref, keep_ref, send_ref, acc_ref):
    core, half = place_ref[0], place_ref[1]
    count, tokens = own_ref.shape[1], own_ref.shape[3]
    width = weight_ref.shape[2]
    for k in range(steps):
        part = slice(k * count // steps, (k + 1) * count // steps)
        columns = slice(k * width // steps, (k + 1) * width // steps)
        block = jnp.concatenate(
            [zip_cores(core, own_ref[t, part], other_ref[t, part]) for t in range(2)],
            axis=1,
        )
        for i in range(2):
            term = jnp.dot(weight_ref[i, :, columns], block, preferred_element_type=F32)
            if k == 0:
                acc_ref[i] = term
            else:
                acc_ref[i] += term
    for i in range(2):
        low, high = acc_ref[i, :, :tokens], acc_ref[i, :, tokens:]
        keep_ref[i] = jnp.where(half == 0, low, high)
        send_ref[i] = jnp.where(half == 0, high, low).astype(BF16)


def up_part(place, own, other, weights, steps=4):
    hidden, width = weights.shape[1:]
    tokens = own.shape[-1]
    own, other = (a.reshape(2, -1, *a.shape[1:]) for a in (own, other))
    vmem = pl.BlockSpec(memory_space=pltpu.VMEM)
    return pl.pallas_call(
        functools.partial(up_kernel, steps),
        in_specs=[pl.BlockSpec(memory_space=pltpu.SMEM), vmem, vmem, vmem],
        out_specs=[vmem, vmem],
        out_shape=[
            jax.ShapeDtypeStruct((2, hidden, tokens), F32),
            jax.ShapeDtypeStruct((2, hidden, tokens), BF16),
        ],
        scratch_shapes=[pltpu.VMEM((2, hidden, 2 * tokens), F32)],
        compiler_params=PARAMS,
        cost_estimate=cost(8 * hidden * width * tokens, 4 * hidden * width + 4 * own.size),
        name="gate_up",
    )(place, own, other, weights)


def down_kernel(place_ref, keep_ref, got_ref, near_ref, far_ref, hidden_ref, mine_ref, theirs_ref):
    side, step = pl.program_id(0), pl.program_id(1)
    core = place_ref[0]

    @pl.when((side == 0) & (step == 0))
    def _():
        preact, uppre = (keep_ref[i] + got_ref[i].astype(F32) for i in range(2))
        hidden_ref[...] = (preact / (1 + jnp.exp(-preact)) * uppre).astype(BF16)

    def part(ref):
        out = jnp.dot(ref[...], hidden_ref[...], preferred_element_type=F32).astype(BF16)
        count, rows, tokens = mine_ref.shape[1:]
        out = out.reshape(count, 2, rows, tokens)
        even, odd = out[:, 0], out[:, 1]
        mine_ref[0] = jnp.where(core == 0, even, odd)
        theirs_ref[0] = jnp.where(core == 0, odd, even)

    pl.when(side == 0)(lambda: part(near_ref))
    pl.when(side == 1)(lambda: part(far_ref))


def down_part(place, keep, got, near, far, rows, steps=2):
    width, hidden = near.shape
    tokens = keep.shape[-1]
    count = width // (2 * rows)
    whole = pl.BlockSpec((2, hidden, tokens), lambda s, k, _: (0, 0, 0))
    block = pl.BlockSpec(
        (1, count // steps, rows, tokens), lambda s, k, p: ((s + p[1]) % 2, k, 0, 0)
    )
    out = jax.ShapeDtypeStruct((2, count, rows, tokens), BF16)
    hidden_units, mine, theirs = pl.pallas_call(
        down_kernel,
        grid_spec=pltpu.PrefetchScalarGridSpec(
            num_scalar_prefetch=1,
            grid=(2, steps),
            in_specs=[
                whole,
                whole,
                pl.BlockSpec((width // steps, hidden), lambda s, k, _: (jnp.where(s == 0, k, steps - 1), 0)),
                pl.BlockSpec((width // steps, hidden), lambda s, k, _: (jnp.where(s == 1, k, 0), 0)),
            ],
            out_specs=[pl.BlockSpec((hidden, tokens), lambda s, k, _: (0, 0)), block, block],
        ),
        out_shape=[jax.ShapeDtypeStruct((hidden, tokens), BF16), out, out],
        compiler_params=PARAMS,
        cost_estimate=cost(0, 0),
        name="down",
    )(place, keep, got, near, far)
    return hidden_units, *(a.reshape(2 * count, rows, tokens) for a in (mine, theirs))


def in_order(core, own_ref, other_ref):
    rows = own_ref.shape[2] // 2
    return jnp.concatenate(
        [
            zip_cores(core, own_ref[y, :, part], other_ref[y, :, part])
            for y in range(own_ref.shape[0])
            for part in (slice(0, rows), slice(rows, 2 * rows))
        ]
    )


def student_kernel(place_ref, own_ref, other_ref, projector_ref, out_ref):
    rows = in_order(place_ref[0], own_ref, other_ref)
    part = jnp.dot(projector_ref[...], rows, preferred_element_type=F32)

    @pl.when(pl.program_id(0) == 0)
    def _():
        out_ref[...] = part

    @pl.when(pl.program_id(0) != 0)
    def _():
        out_ref[...] += part


def student_part(place, own, other, projector, steps=4):
    across, count, rows, tokens = own.shape
    mine, width = projector.shape
    block = pl.BlockSpec((across // steps, count, rows, tokens), lambda k, _: (k, 0, 0, 0))
    return pl.pallas_call(
        student_kernel,
        grid_spec=pltpu.PrefetchScalarGridSpec(
            num_scalar_prefetch=1,
            grid=(steps,),
            in_specs=[block, block, pl.BlockSpec((mine, width // steps), lambda k, _: (0, k))],
            out_specs=pl.BlockSpec((mine, tokens), lambda k, _: (0, 0)),
        ),
        out_shape=jax.ShapeDtypeStruct((mine, tokens), F32),
        compiler_params=PARAMS,
        cost_estimate=cost(2 * mine * width * tokens, 2 * width * tokens + 2 * mine * width),
        name="student",
    )(place, own, other, projector)


def grad_kernel(place_ref, terms_ref, student_out_ref, own_ref, other_ref, residual_ref, grad_ref):
    @pl.when(pl.program_id(0) == 0)
    def _():
        teacher_out = jnp.sum(terms_ref[...].astype(F32), axis=0)
        residual_ref[...] = (student_out_ref[...] - teacher_out).astype(BF16)

    rows = in_order(place_ref[0], own_ref, other_ref)
    grad_ref[...] = lax.dot_general(
        residual_ref[...], rows, (((1,), (1,)), ((), ())), preferred_element_type=F32
    ).astype(BF16)


def grad_part(place, terms, student_out, own, other, steps=4):
    mine, tokens = student_out.shape
    across, count, rows = own.shape[:3]
    width = 2 * across * count * rows
    small = pl.BlockSpec((mine, tokens), lambda k, _: (0, 0))
    block = pl.BlockSpec((across // steps, count, rows, tokens), lambda k, _: (k, 0, 0, 0))
    return pl.pallas_call(
        grad_kernel,
        grid_spec=pltpu.PrefetchScalarGridSpec(
            num_scalar_prefetch=1,
            grid=(steps,),
            in_specs=[pl.BlockSpec(terms.shape, lambda k, _: (0, 0, 0)), small, block, block],
            out_specs=[small, pl.BlockSpec((mine, width // steps), lambda k, _: (0, k))],
        ),
        out_shape=[
            jax.ShapeDtypeStruct((mine, tokens), BF16),
            jax.ShapeDtypeStruct((mine, width), BF16),
        ],
        compiler_params=PARAMS,
        cost_estimate=cost(2 * mine * width * tokens, 2 * (terms.size + width * tokens + mine * width)),
        name="gradient",
    )(place, terms, student_out, own, other)


def shards(teacher_rows, teacher_gate, teacher_up, teacher_down, student_rows, projector):
    place = jnp.stack([lax.axis_index(name) for name in ("core", "dp")]).astype(jnp.int32)
    rows = teacher_rows.shape[0]
    chips = lax.axis_size(CHIPS)
    across = lax.axis_size("y") // 2
    spread = functools.partial(lax.all_to_all, split_axis=0, concat_axis=0, tiled=True)

    trade = []
    for y in range(across):
        low, high = 2 * y, 2 * (y + across)
        trade += [(low, low), (low + 1, high), (high, low + 1), (high + 1, high + 1)]
    held = lax.ppermute(teacher_rows, ("y", "dp"), trade)
    near_x = lax.ppermute(student_rows, "x", SWAP)
    held, near_x = lax.optimization_barrier((held, near_x))
    first = lax.axis_index("x") == 0
    pair = jnp.concatenate(
        [jnp.where(first, student_rows, near_x), jnp.where(first, near_x, student_rows)]
    )
    down_far = lax.ppermute(teacher_down, "dp", SWAP)
    plane = ("y", "z")
    teacher_own = spread(copies(held, held, chips), CHIPS)
    teacher_own, down_far, down_near, student_copies, gate_and_up = lax.optimization_barrier(
        (
            teacher_own,
            down_far,
            teacher_down.T,
            copies(pair, held, lax.axis_size(plane)),
            pack(teacher_gate, teacher_up),
        )
    )
    teacher_other = lax.ppermute(teacher_own, "core", SWAP)
    student_own = spread(student_copies, plane)

    keep, send = up_part(place, teacher_own, teacher_other, gate_and_up)
    send, down_far = lax.optimization_barrier((send, down_far))
    got = lax.ppermute(send, "dp", SWAP)
    teacher_hidden, mine, theirs = down_part(place, keep, got, down_near, down_far.T, rows)
    chip_sum = (
        mine.astype(F32) + lax.ppermute(theirs, "core", SWAP).astype(F32)
    ).astype(BF16)
    terms = spread(chip_sum, CHIPS)

    student_other = lax.ppermute(student_own, "core", SWAP)
    student_own, student_other = (
        a.reshape(lax.axis_size("y"), -1, *a.shape[1:]) for a in (student_own, student_other)
    )
    student_out = student_part(place, student_own, student_other, projector)
    residual_error, grad_local = grad_part(place, terms, student_out, student_own, student_other)
    grad_projector = grad_local + lax.ppermute(grad_local, "dp", SWAP)
    return (teacher_hidden, residual_error, grad_projector)


def solution(mesh):
    fine = Mesh(mesh.devices.reshape(8, 2, 8, 2, 2), (*CHIPS, "core", "dp"))
    blk = (*CHIPS, "core")
    return jax.shard_map(
        shards,
        mesh=fine,
        in_specs=(P(blk, "dp"),) * 5 + (P(blk, None),),
        out_specs=(P(blk, "dp"), P(blk, "dp"), P(blk, None)),
        check_vma=False,
    )
```

```python
import functools

import jax
import jax.numpy as jnp
from jax import lax
from jax.experimental import pallas as pl
from jax.experimental.pallas import tpu as pltpu
from jax.sharding import Mesh, PartitionSpec as P

CHIPS = ("y", "x", "z")
SWAP = [(0, 1), (1, 0)]
F32, BF16 = jnp.float32, jnp.bfloat16
PARAMS = pltpu.CompilerParams(vmem_limit_bytes=24 << 20)


def cost(flops, size):
    return pl.CostEstimate(flops=flops, bytes_accessed=size, transcendentals=0)


def zip_cores(core, own, other):
    count, rows, tokens = own.shape
    even = jnp.where(core == 0, own, other)
    odd = jnp.where(core == 0, other, own)
    return jnp.stack([even, odd], axis=1).reshape(count * 2 * rows, tokens)


def copies_kernel(place_ref, mine_ref, next_ref, out_ref):
    rows = mine_ref.shape[0]
    shape = (out_ref.shape[0], *mine_ref.shape)
    even = place_ref[2] == 0
    mine, other = mine_ref[...], next_ref[...]
    out_ref[:, :rows] = jnp.broadcast_to(jnp.where(even, mine, other)[None], shape)
    out_ref[:, rows:] = jnp.broadcast_to(jnp.where(even, other, mine)[None], shape)


def copies(place, mine, next_x, count):
    rows, tokens = mine.shape
    vmem = pl.BlockSpec(memory_space=pltpu.VMEM)
    return pl.pallas_call(
        copies_kernel,
        in_specs=[pl.BlockSpec(memory_space=pltpu.SMEM), vmem, vmem],
        out_specs=vmem,
        out_shape=jax.ShapeDtypeStruct((count, 2 * rows, tokens), BF16),
        compiler_params=PARAMS,
        cost_estimate=cost(0, 4 * count * rows * tokens),
        name="copies",
    )(place, mine, next_x)


def pack_kernel(gate_ref, up_ref, out_ref):
    out_ref[0] = gate_ref[...]
    out_ref[1] = up_ref[...]


def pack(gate, up, steps=4):
    hidden, width = gate.shape
    block = pl.BlockSpec((hidden, width // steps), lambda k: (0, k))
    return pl.pallas_call(
        pack_kernel,
        grid=(steps,),
        in_specs=[block, block],
        out_specs=pl.BlockSpec((2, hidden, width // steps), lambda k: (0, 0, k)),
        out_shape=jax.ShapeDtypeStruct((2, hidden, width), BF16),
        compiler_params=PARAMS,
        cost_estimate=cost(0, 8 * hidden * width),
        name="pack",
    )(gate, up)


def in_order(core, own_ref, other_ref):
    rows = own_ref.shape[2] // 2
    return jnp.concatenate(
        [
            zip_cores(core, own_ref[y, :, part], other_ref[y, :, part])
            for y in range(own_ref.shape[0])
            for part in (slice(0, rows), slice(rows, 2 * rows))
        ]
    )


def up_kernel(place_ref, own_ref, other_ref, weight_ref, keep_ref, send_ref, acc_ref):
    core, half = place_ref[0], place_ref[1]
    steps, tokens = own_ref.shape[1], own_ref.shape[4]
    width = weight_ref.shape[2] // steps
    for k in range(steps):
        part = pl.ds(k, 1)
        block = jnp.concatenate(
            [in_order(core, own_ref.at[t, part], other_ref.at[t, part]) for t in range(2)], axis=1
        )
        for i in range(2):
            columns = slice(k * width, (k + 1) * width)
            term = jnp.dot(weight_ref[i, :, columns], block, preferred_element_type=F32)
            if k == 0:
                acc_ref[i] = term
            else:
                acc_ref[i] += term
    for i in range(2):
        low, high = acc_ref[i, :, :tokens], acc_ref[i, :, tokens:]
        keep_ref[i] = jnp.where(half == 0, low, high)
        send_ref[i] = jnp.where(half == 0, high, low).astype(BF16)


def up_part(place, own, other, weights):
    hidden, width = weights.shape[1:]
    tokens = own.shape[-1]
    own, other = (a.reshape(2, -1, *a.shape[1:]) for a in (own, other))
    vmem = pl.BlockSpec(memory_space=pltpu.VMEM)
    return pl.pallas_call(
        up_kernel,
        in_specs=[pl.BlockSpec(memory_space=pltpu.SMEM), vmem, vmem, vmem],
        out_specs=[vmem, vmem],
        out_shape=[
            jax.ShapeDtypeStruct((2, hidden, tokens), F32),
            jax.ShapeDtypeStruct((2, hidden, tokens), BF16),
        ],
        scratch_shapes=[pltpu.VMEM((2, hidden, 2 * tokens), F32)],
        compiler_params=PARAMS,
        cost_estimate=cost(8 * hidden * width * tokens, 4 * hidden * width + 4 * own.size),
        name="gate_up",
    )(place, own, other, weights)


def down_kernel(place_ref, keep_ref, got_ref, near_ref, far_low_ref, far_high_ref, hidden_ref, mine_ref, theirs_ref):
    side, step = pl.program_id(0), pl.program_id(1)
    core = place_ref[0]

    @pl.when((side == 0) & (step == 0))
    def _():
        preact, uppre = (keep_ref[i] + got_ref[i].astype(F32) for i in range(2))
        hidden_ref[...] = (preact / (1 + jnp.exp(-preact)) * uppre).astype(BF16)

    def part(*refs):
        out, row = 0, 0
        for ref in refs:
            units = hidden_ref[row : row + ref.shape[1]]
            out += jnp.dot(ref[...], units, preferred_element_type=F32)
            row += ref.shape[1]
        out = out.astype(BF16)
        count, rows, tokens = mine_ref.shape[1:]
        out = out.reshape(count, 2, rows, tokens)
        even, odd = out[:, 0], out[:, 1]
        mine_ref[0] = jnp.where(core == 0, even, odd)
        theirs_ref[0] = jnp.where(core == 0, odd, even)

    pl.when(side == 0)(lambda: part(near_ref))
    pl.when(side == 1)(lambda: part(far_low_ref, far_high_ref))


def down_part(place, keep, got, near, far_low, far_high, rows, steps=2):
    width, hidden = near.shape
    tokens = keep.shape[-1]
    count = width // (2 * rows)
    whole = pl.BlockSpec((2, hidden, tokens), lambda s, k, _: (0, 0, 0))
    block = pl.BlockSpec(
        (1, count // steps, rows, tokens), lambda s, k, p: ((s + p[1]) % 2, k, 0, 0)
    )
    out = jax.ShapeDtypeStruct((2, count, rows, tokens), BF16)
    hidden_units, mine, theirs = pl.pallas_call(
        down_kernel,
        grid_spec=pltpu.PrefetchScalarGridSpec(
            num_scalar_prefetch=1,
            grid=(2, steps),
            in_specs=[
                whole,
                whole,
                pl.BlockSpec((width // steps, hidden), lambda s, k, _: (jnp.where(s == 0, k, steps - 1), 0)),
                *(
                    pl.BlockSpec(
                        (width // steps, far.shape[1]), lambda s, k, _: (jnp.where(s == 1, k, 0), 0)
                    )
                    for far in (far_low, far_high)
                ),
            ],
            out_specs=[pl.BlockSpec((hidden, tokens), lambda s, k, _: (0, 0)), block, block],
        ),
        out_shape=[jax.ShapeDtypeStruct((hidden, tokens), BF16), out, out],
        compiler_params=PARAMS,
        cost_estimate=cost(0, 0),
        name="down",
    )(place, keep, got, near, far_low, far_high)
    return hidden_units, *(a.reshape(2 * count, rows, tokens) for a in (mine, theirs))


def student_kernel(place_ref, own_ref, other_ref, projector_ref, out_ref):
    rows = in_order(place_ref[0], own_ref, other_ref)
    part = jnp.dot(projector_ref[...], rows, preferred_element_type=F32)

    @pl.when(pl.program_id(0) == 0)
    def _():
        out_ref[...] = part

    @pl.when(pl.program_id(0) != 0)
    def _():
        out_ref[...] += part


def student_part(place, own, other, projector, steps=4):
    across, count, rows, tokens = own.shape
    mine, width = projector.shape
    block = pl.BlockSpec((across // steps, count, rows, tokens), lambda k, _: (k, 0, 0, 0))
    return pl.pallas_call(
        student_kernel,
        grid_spec=pltpu.PrefetchScalarGridSpec(
            num_scalar_prefetch=1,
            grid=(steps,),
            in_specs=[block, block, pl.BlockSpec((mine, width // steps), lambda k, _: (0, k))],
            out_specs=pl.BlockSpec((mine, tokens), lambda k, _: (0, 0)),
        ),
        out_shape=jax.ShapeDtypeStruct((mine, tokens), F32),
        compiler_params=PARAMS,
        cost_estimate=cost(2 * mine * width * tokens, 2 * width * tokens + 2 * mine * width),
        name="student",
    )(place, own, other, projector)


def grad_kernel(place_ref, terms_ref, student_out_ref, own_ref, other_ref, residual_ref, grad_ref):
    @pl.when(pl.program_id(0) == 0)
    def _():
        teacher_out = jnp.sum(terms_ref[...].astype(F32), axis=0)
        residual_ref[...] = (student_out_ref[...] - teacher_out).astype(BF16)

    rows = in_order(place_ref[0], own_ref, other_ref)
    grad_ref[...] = lax.dot_general(
        residual_ref[...], rows, (((1,), (1,)), ((), ())), preferred_element_type=F32
    ).astype(BF16)


def grad_part(place, terms, student_out, own, other, steps=4):
    mine, tokens = student_out.shape
    across, count, rows = own.shape[:3]
    width = 2 * across * count * rows
    small = pl.BlockSpec((mine, tokens), lambda k, _: (0, 0))
    block = pl.BlockSpec((across // steps, count, rows, tokens), lambda k, _: (k, 0, 0, 0))
    return pl.pallas_call(
        grad_kernel,
        grid_spec=pltpu.PrefetchScalarGridSpec(
            num_scalar_prefetch=1,
            grid=(steps,),
            in_specs=[pl.BlockSpec(terms.shape, lambda k, _: (0, 0, 0)), small, block, block],
            out_specs=[small, pl.BlockSpec((mine, width // steps), lambda k, _: (0, k))],
        ),
        out_shape=[
            jax.ShapeDtypeStruct((mine, tokens), BF16),
            jax.ShapeDtypeStruct((mine, width), BF16),
        ],
        compiler_params=PARAMS,
        cost_estimate=cost(2 * mine * width * tokens, 2 * (terms.size + width * tokens + mine * width)),
        name="gradient",
    )(place, terms, student_out, own, other)


def shards(teacher_rows, teacher_gate, teacher_up, teacher_down, student_rows, projector):
    place = jnp.stack([lax.axis_index(name) for name in ("core", "dp", "x")]).astype(jnp.int32)
    rows = teacher_rows.shape[0]
    plane = ("y", "z")
    peers = lax.axis_size(plane)
    across = lax.axis_size("y") // 2
    spread = functools.partial(lax.all_to_all, split_axis=0, concat_axis=0, tiled=True)

    trade, trade_x = [], []
    for y in range(2 * across):
        for d in range(2):
            low = y < across
            to = (y, d) if low == (d == 0) else (y + across if low else y - across, 1 - d)
            for x in range(2):
                trade.append(((y * 2 + x) * 2 + d, (to[0] * 2 + x) * 2 + to[1]))
                trade_x.append(((y * 2 + x) * 2 + d, (to[0] * 2 + 1 - x) * 2 + to[1]))
    held, held_x = (lax.ppermute(teacher_rows, ("y", "x", "dp"), t) for t in (trade, trade_x))
    near_x = lax.ppermute(student_rows, "x", SWAP)
    held, held_x, near_x = lax.optimization_barrier((held, held_x, near_x))
    units = 48
    far_low = lax.ppermute(teacher_down[:units], "dp", SWAP)
    teacher_own = spread(copies(place, held, held_x, peers), plane)
    teacher_own, far_low, down_near, student_copies, gate_and_up = lax.optimization_barrier(
        (
            teacher_own,
            far_low,
            teacher_down.T,
            copies(place, student_rows, near_x, peers),
            pack(teacher_gate, teacher_up),
        )
    )
    by_y = lambda a: a.reshape(2 * across, -1, *a.shape[1:])
    teacher_other = lax.ppermute(teacher_own, "core", SWAP)
    far_high = lax.ppermute(teacher_down[units:], "dp", SWAP)
    student_own = spread(student_copies, plane)

    keep, send = up_part(place, by_y(teacher_own), by_y(teacher_other), gate_and_up)
    send, far_low = lax.optimization_barrier((send, far_low))
    got = lax.ppermute(send, "dp", SWAP)
    teacher_hidden, mine, theirs = down_part(place, keep, got, down_near, far_low.T, far_high.T, rows)
    chip_sum = (
        mine.astype(F32) + lax.ppermute(theirs, "core", SWAP).astype(F32)
    ).astype(BF16)
    terms = spread(chip_sum, CHIPS)

    student_other = lax.ppermute(student_own, "core", SWAP)
    student_own, student_other = (
        a.reshape(lax.axis_size("y"), -1, *a.shape[1:]) for a in (student_own, student_other)
    )
    student_out = student_part(place, student_own, student_other, projector)
    residual_error, grad_local = grad_part(place, terms, student_out, student_own, student_other)
    grad_projector = grad_local + lax.ppermute(grad_local, "dp", SWAP)
    return (teacher_hidden, residual_error, grad_projector)


def solution(mesh):
    fine = Mesh(mesh.devices.reshape(8, 2, 8, 2, 2), (*CHIPS, "core", "dp"))
    blk = (*CHIPS, "core")
    return jax.shard_map(
        shards,
        mesh=fine,
        in_specs=(P(blk, "dp"),) * 5 + (P(blk, None),),
        out_specs=(P(blk, "dp"), P(blk, "dp"), P(blk, None)),
        check_vma=False,
    )
```

```python
import functools

import jax
import jax.numpy as jnp
from jax import lax
from jax.experimental import pallas as pl
from jax.experimental.pallas import tpu as pltpu
from jax.sharding import Mesh, PartitionSpec as P

CHIPS = ("y", "x", "z")
SWAP = [(0, 1), (1, 0)]
F32, BF16 = jnp.float32, jnp.bfloat16
PARAMS = pltpu.CompilerParams(vmem_limit_bytes=24 << 20)


def cost(flops, size):
    return pl.CostEstimate(flops=flops, bytes_accessed=size, transcendentals=0)


def zip_cores(core, own, other):
    count, rows, tokens = own.shape
    even = jnp.where(core == 0, own, other)
    odd = jnp.where(core == 0, other, own)
    return jnp.stack([even, odd], axis=1).reshape(count * 2 * rows, tokens)


def copies_kernel(place_ref, mine_ref, next_ref, out_ref):
    rows = mine_ref.shape[0]
    shape = (out_ref.shape[0], *mine_ref.shape)
    even = place_ref[2] == 0
    mine, other = mine_ref[...], next_ref[...]
    out_ref[:, :rows] = jnp.broadcast_to(jnp.where(even, mine, other)[None], shape)
    out_ref[:, rows:] = jnp.broadcast_to(jnp.where(even, other, mine)[None], shape)


def copies(place, mine, next_x, count):
    rows, tokens = mine.shape
    vmem = pl.BlockSpec(memory_space=pltpu.VMEM)
    return pl.pallas_call(
        copies_kernel,
        in_specs=[pl.BlockSpec(memory_space=pltpu.SMEM), vmem, vmem],
        out_specs=vmem,
        out_shape=jax.ShapeDtypeStruct((count, 2 * rows, tokens), BF16),
        compiler_params=PARAMS,
        cost_estimate=cost(0, 4 * count * rows * tokens),
        name="copies",
    )(place, mine, next_x)


def pack_kernel(gate_ref, up_ref, out_ref):
    out_ref[0] = gate_ref[...]
    out_ref[1] = up_ref[...]


def pack(gate, up, steps=4):
    hidden, width = gate.shape
    block = pl.BlockSpec((hidden, width // steps), lambda k: (0, k))
    return pl.pallas_call(
        pack_kernel,
        grid=(steps,),
        in_specs=[block, block],
        out_specs=pl.BlockSpec((2, hidden, width // steps), lambda k: (0, 0, k)),
        out_shape=jax.ShapeDtypeStruct((2, hidden, width), BF16),
        compiler_params=PARAMS,
        cost_estimate=cost(0, 8 * hidden * width),
        name="pack",
    )(gate, up)


def in_order(core, own_ref, other_ref):
    rows = own_ref.shape[2] // 2
    return jnp.concatenate(
        [
            zip_cores(core, own_ref[y, :, part], other_ref[y, :, part])
            for y in range(own_ref.shape[0])
            for part in (slice(0, rows), slice(rows, 2 * rows))
        ]
    )


def up_kernel(place_ref, own_ref, other_ref, weight_ref, keep_ref, send_ref, acc_ref):
    core, half = place_ref[0], place_ref[1]
    steps, tokens = own_ref.shape[1], own_ref.shape[4]
    width = weight_ref.shape[2] // steps
    for k in range(steps):
        part = pl.ds(k, 1)
        block = jnp.concatenate(
            [in_order(core, own_ref.at[t, part], other_ref.at[t, part]) for t in range(2)], axis=1
        )
        for i in range(2):
            columns = slice(k * width, (k + 1) * width)
            term = jnp.dot(weight_ref[i, :, columns], block, preferred_element_type=F32)
            if k == 0:
                acc_ref[i] = term
            else:
                acc_ref[i] += term
    for i in range(2):
        low, high = acc_ref[i, :, :tokens], acc_ref[i, :, tokens:]
        keep_ref[i] = jnp.where(half == 0, low, high)
        send_ref[i] = jnp.where(half == 0, high, low).astype(BF16)


def up_part(place, own, other, weights):
    hidden, width = weights.shape[1:]
    tokens = own.shape[-1]
    own, other = (a.reshape(2, -1, *a.shape[1:]) for a in (own, other))
    vmem = pl.BlockSpec(memory_space=pltpu.VMEM)
    return pl.pallas_call(
        up_kernel,
        in_specs=[pl.BlockSpec(memory_space=pltpu.SMEM), vmem, vmem, vmem],
        out_specs=[vmem, vmem],
        out_shape=[
            jax.ShapeDtypeStruct((2, hidden, tokens), F32),
            jax.ShapeDtypeStruct((2, hidden, tokens), BF16),
        ],
        scratch_shapes=[pltpu.VMEM((2, hidden, 2 * tokens), F32)],
        compiler_params=PARAMS,
        cost_estimate=cost(8 * hidden * width * tokens, 4 * hidden * width + 4 * own.size),
        name="gate_up",
    )(place, own, other, weights)


def down_kernel(place_ref, keep_ref, got_ref, near_ref, far_low_ref, far_high_ref, hidden_ref, mine_ref, theirs_ref):
    side, step = pl.program_id(0), pl.program_id(1)
    core = place_ref[0]

    @pl.when((side == 0) & (step == 0))
    def _():
        preact, uppre = (keep_ref[i] + got_ref[i].astype(F32) for i in range(2))
        hidden_ref[...] = (preact / (1 + jnp.exp(-preact)) * uppre).astype(BF16)

    def part(*refs):
        out, row = 0, 0
        for ref in refs:
            units = hidden_ref[row : row + ref.shape[1]]
            out += jnp.dot(ref[...], units, preferred_element_type=F32)
            row += ref.shape[1]
        out = out.astype(BF16)
        count, rows, tokens = mine_ref.shape[1:]
        out = out.reshape(count, 2, rows, tokens)
        even, odd = out[:, 0], out[:, 1]
        mine_ref[0] = jnp.where(core == 0, even, odd)
        theirs_ref[0] = jnp.where(core == 0, odd, even)

    pl.when(side == 0)(lambda: part(near_ref))
    pl.when(side == 1)(lambda: part(far_low_ref, far_high_ref))


def down_part(place, keep, got, near, far_low, far_high, rows, steps=2):
    width, hidden = near.shape
    tokens = keep.shape[-1]
    count = width // (2 * rows)
    whole = pl.BlockSpec((2, hidden, tokens), lambda s, k, _: (0, 0, 0))
    block = pl.BlockSpec(
        (1, count // steps, rows, tokens), lambda s, k, p: ((s + p[1]) % 2, k, 0, 0)
    )
    out = jax.ShapeDtypeStruct((2, count, rows, tokens), BF16)
    hidden_units, mine, theirs = pl.pallas_call(
        down_kernel,
        grid_spec=pltpu.PrefetchScalarGridSpec(
            num_scalar_prefetch=1,
            grid=(2, steps),
            in_specs=[
                whole,
                whole,
                pl.BlockSpec((width // steps, hidden), lambda s, k, _: (jnp.where(s == 0, k, steps - 1), 0)),
                *(
                    pl.BlockSpec(
                        (width // steps, far.shape[1]), lambda s, k, _: (jnp.where(s == 1, k, 0), 0)
                    )
                    for far in (far_low, far_high)
                ),
            ],
            out_specs=[pl.BlockSpec((hidden, tokens), lambda s, k, _: (0, 0)), block, block],
        ),
        out_shape=[jax.ShapeDtypeStruct((hidden, tokens), BF16), out, out],
        compiler_params=PARAMS,
        cost_estimate=cost(0, 0),
        name="down",
    )(place, keep, got, near, far_low, far_high)
    return hidden_units, *(a.reshape(2 * count, rows, tokens) for a in (mine, theirs))


def student_kernel(place_ref, own_ref, other_ref, projector_ref, out_ref):
    rows = in_order(place_ref[0], own_ref, other_ref)
    part = jnp.dot(projector_ref[...], rows, preferred_element_type=F32)

    @pl.when(pl.program_id(0) == 0)
    def _():
        out_ref[...] = part

    @pl.when(pl.program_id(0) != 0)
    def _():
        out_ref[...] += part


def student_part(place, own, other, projector, steps=4):
    across, count, rows, tokens = own.shape
    mine, width = projector.shape
    block = pl.BlockSpec((across // steps, count, rows, tokens), lambda k, _: (k, 0, 0, 0))
    return pl.pallas_call(
        student_kernel,
        grid_spec=pltpu.PrefetchScalarGridSpec(
            num_scalar_prefetch=1,
            grid=(steps,),
            in_specs=[block, block, pl.BlockSpec((mine, width // steps), lambda k, _: (0, k))],
            out_specs=pl.BlockSpec((mine, tokens), lambda k, _: (0, 0)),
        ),
        out_shape=jax.ShapeDtypeStruct((mine, tokens), F32),
        compiler_params=PARAMS,
        cost_estimate=cost(2 * mine * width * tokens, 2 * width * tokens + 2 * mine * width),
        name="student",
    )(place, own, other, projector)


def grad_kernel(place_ref, terms_ref, student_out_ref, own_ref, other_ref, residual_ref, grad_ref):
    @pl.when(pl.program_id(0) == 0)
    def _():
        teacher_out = jnp.sum(terms_ref[...].astype(F32), axis=0)
        residual_ref[...] = (student_out_ref[...] - teacher_out).astype(BF16)

    rows = in_order(place_ref[0], own_ref, other_ref)
    grad_ref[...] = lax.dot_general(
        residual_ref[...], rows, (((1,), (1,)), ((), ())), preferred_element_type=F32
    ).astype(BF16)


def grad_part(place, terms, student_out, own, other, steps=4):
    mine, tokens = student_out.shape
    across, count, rows = own.shape[:3]
    width = 2 * across * count * rows
    small = pl.BlockSpec((mine, tokens), lambda k, _: (0, 0))
    block = pl.BlockSpec((across // steps, count, rows, tokens), lambda k, _: (k, 0, 0, 0))
    return pl.pallas_call(
        grad_kernel,
        grid_spec=pltpu.PrefetchScalarGridSpec(
            num_scalar_prefetch=1,
            grid=(steps,),
            in_specs=[pl.BlockSpec(terms.shape, lambda k, _: (0, 0, 0)), small, block, block],
            out_specs=[small, pl.BlockSpec((mine, width // steps), lambda k, _: (0, k))],
        ),
        out_shape=[
            jax.ShapeDtypeStruct((mine, tokens), BF16),
            jax.ShapeDtypeStruct((mine, width), BF16),
        ],
        compiler_params=PARAMS,
        cost_estimate=cost(2 * mine * width * tokens, 2 * (terms.size + width * tokens + mine * width)),
        name="gradient",
    )(place, terms, student_out, own, other)


def shards(teacher_rows, teacher_gate, teacher_up, teacher_down, student_rows, projector):
    place = jnp.stack([lax.axis_index(name) for name in ("core", "dp", "x")]).astype(jnp.int32)
    rows = teacher_rows.shape[0]
    plane = ("y", "z")
    peers = lax.axis_size(plane)
    across = lax.axis_size("y") // 2
    spread = functools.partial(lax.all_to_all, split_axis=0, concat_axis=0, tiled=True)

    trade, trade_x = [], []
    for y in range(2 * across):
        for d in range(2):
            low = y < across
            to = (y, d) if low == (d == 0) else (y + across if low else y - across, 1 - d)
            for x in range(2):
                trade.append(((y * 2 + x) * 2 + d, (to[0] * 2 + x) * 2 + to[1]))
                trade_x.append(((y * 2 + x) * 2 + d, (to[0] * 2 + 1 - x) * 2 + to[1]))
    held, held_x = (lax.ppermute(teacher_rows, ("y", "x", "dp"), t) for t in (trade, trade_x))
    near_x = lax.ppermute(student_rows, "x", SWAP)
    held, held_x, near_x = lax.optimization_barrier((held, held_x, near_x))
    units = 80
    far_low = lax.ppermute(teacher_down[:units], "dp", SWAP)
    teacher_own = spread(copies(place, held, held_x, peers), plane)
    teacher_own, far_low, down_near, student_copies, gate_and_up = lax.optimization_barrier(
        (
            teacher_own,
            far_low,
            teacher_down.T,
            copies(place, student_rows, near_x, peers),
            pack(teacher_gate, teacher_up),
        )
    )
    by_y = lambda a: a.reshape(2 * across, -1, *a.shape[1:])
    teacher_other = lax.ppermute(teacher_own, "core", SWAP)
    far_high = lax.ppermute(teacher_down[units:], "dp", SWAP)
    student_own = spread(student_copies, plane)

    keep, send = up_part(place, by_y(teacher_own), by_y(teacher_other), gate_and_up)
    send, far_low = lax.optimization_barrier((send, far_low))
    got = lax.ppermute(send, "dp", SWAP)
    teacher_hidden, mine, theirs = down_part(place, keep, got, down_near, far_low.T, far_high.T, rows)
    chip_sum = (
        mine.astype(F32) + lax.ppermute(theirs, "core", SWAP).astype(F32)
    ).astype(BF16)
    terms = spread(chip_sum, CHIPS)

    student_other = lax.ppermute(student_own, "core", SWAP)
    student_own, student_other = (
        a.reshape(lax.axis_size("y"), -1, *a.shape[1:]) for a in (student_own, student_other)
    )
    student_out = student_part(place, student_own, student_other, projector)
    residual_error, grad_local = grad_part(place, terms, student_out, student_own, student_other)
    grad_projector = grad_local + lax.ppermute(grad_local, "dp", SWAP)
    return (teacher_hidden, residual_error, grad_projector)


def solution(mesh):
    fine = Mesh(mesh.devices.reshape(8, 2, 8, 2, 2), (*CHIPS, "core", "dp"))
    blk = (*CHIPS, "core")
    return jax.shard_map(
        shards,
        mesh=fine,
        in_specs=(P(blk, "dp"),) * 5 + (P(blk, None),),
        out_specs=(P(blk, "dp"), P(blk, "dp"), P(blk, None)),
        check_vma=False,
    )
```
